128 devices in a mesh: seq: 16 (over x, y_hi, core), expert: 4 (over z), dp: 2 (over y_lo).
Axes of the slice: x: 4, y: 4 (y_hi: 2, y_lo: 2; y = y_hi * 2 + y_lo), z: 4, core: 2. Of those that a mesh axis runs over, the one named last changes fastest.
Arguments:
- queries: bfloat16 [32, 512, 1024], P(('expert', 'dp'), 'seq'), may hold values from -6 to 6
- memory_keys: bfloat16 [32, 2048, 1024], P(('expert', 'dp'), 'seq'), may hold values from -6 to 6
- memory_values: bfloat16 [32, 2048, 1024], P(('expert', 'dp'), 'seq'), may hold values from -6 to 6
- stream: bfloat16 [32, 512, 1024], P(('expert', 'dp'), 'seq'), may hold values from -36 to 36
- norm_gain: float32 [1024], replicated, may hold values from 0.1 to 1.9
- gate_proj: bfloat16 [32, 1024, 2816], P('seq', None, ('expert', 'dp')), may hold values from -0.1875 to 0.1875
- up_proj: bfloat16 [32, 1024, 2816], P('seq', None, ('expert', 'dp')), may hold values from -0.1875 to 0.1875
- down_proj: bfloat16 [32, 2816, 1024], P('seq', ('expert', 'dp')), may hold values from -0.109375 to 0.109375
- expert_ids: int32 [16, 8, 128, 2], P('seq', ('expert', 'dp')), may hold values from 0 to 31, all different within a row; in each aligned block of 128 rows (0 to 127, 128 to 255, ..., all dimensions but the last counted through in order) at most 12 rows name the same one
- gate_weights: bfloat16 [16, 8, 128, 2], P('seq', ('expert', 'dp')), may hold values from 0.099609375 to 0.8984375
- upstream_grad: bfloat16 [32, 512, 1024], P(('expert', 'dp'), 'seq'), may hold values from -6 to 6
Outputs:
- queries_grad: bfloat16 [32, 512, 1024], P(('expert', 'dp'), 'seq')
- keys_grad: bfloat16 [32, 2048, 1024], P(('expert', 'dp'), 'seq')
- values_grad: bfloat16 [32, 2048, 1024], P(('expert', 'dp'), 'seq')
- stream_grad: bfloat16 [32, 512, 1024], P(('expert', 'dp'), 'seq')
- gain_grad: float32 [1024], replicated
- gate_proj_grad: bfloat16 [32, 1024, 2816], P('seq', None, ('expert', 'dp'))
- up_proj_grad: bfloat16 [32, 1024, 2816], P('seq', None, ('expert', 'dp'))
- down_proj_grad: bfloat16 [32, 2816, 1024], P('seq', ('expert', 'dp'))
- gate_weights_grad: float32 [16, 8, 128, 2], P('seq', ('expert', 'dp'))
The draws below stay inside these ranges and needn't reach their ends.
Inputs may be any that keep to these rules, and one draw needn't show every extreme that they name: `expert_ids`: in the block of 128 tokens of one index (s, g) no expert is named by more than 12 of the 256 choices; the two choices of a token differ.
All inputs are finite; a program needn't handle non-finite values.
Results may differ from the reference program's by a relative error of at most 0.01355.
Values may be sent and summed in bfloat16 or wider, within the bound.
No kernel may reach another device: no remote copies, remote signals or barrier semaphores. Data moves between devices by JAX's collectives and lax.ppermute only.
A program may use at most 256 MiB of HBM per device.

```python
import math
import jax
import jax.numpy as jnp
import numpy as np
from jax import lax

D = 1024
HEADS = 16
FF = 2816
DEC_DEV = 32
TOK_DEV = 128
EX_DEV = 4
HD = 64
LDEC = 512
LMEM = 2048
GROUPS = 8
BATCH = 32
EXPERTS = 32
CAP = 12
N_SEQ = 16
N_EXPERT = 4
N_DP = 2


def draw_queries(key, part):
    key = jax.random.fold_in(key, 21)
    sample = jnp.clip(jax.random.normal(key, (BATCH, LDEC, D), jnp.float32), -4.0, 4.0)
    return sample.astype(jnp.bfloat16)


def draw_memory_keys(key, part):
    key = jax.random.fold_in(key, 22)
    sample = jnp.clip(jax.random.normal(key, (BATCH, LMEM, D), jnp.float32), -4.0, 4.0)
    return sample.astype(jnp.bfloat16)


def draw_stream(key, part):
    key = jax.random.fold_in(key, 23)
    base_key, row_key, column_key = jax.random.split(key, 3)
    row_scale = jnp.exp(jax.random.uniform(row_key, (BATCH, LDEC, 1), jnp.float32, -1.2, 1.1))
    column_scale = jnp.exp(jax.random.uniform(column_key, (1, 1, D), jnp.float32, -1.2, 1.1))
    sample = jnp.clip(jax.random.normal(base_key, (BATCH, LDEC, D), jnp.float32), -4.0, 4.0)
    return (sample * row_scale * column_scale).astype(jnp.bfloat16)


def block_scale(stream_key, dims, cuts, low, largest):
    factor_of, own = 1.0, jax.random.fold_in(stream_key, 6)
    for axis_at, parts in cuts:
        steps = jnp.exp(jax.random.uniform(jax.random.fold_in(own, axis_at), (parts,), jnp.float32, low / len(cuts), largest / len(cuts)))
        factor_of = factor_of * jnp.repeat(steps, dims[axis_at] // parts).reshape([-1 if axis == axis_at else 1 for axis in range(len(dims))])
    return factor_of


def assign_block(rng, own, number, rows, count, top, most, lean):
    ranking = jax.random.permutation(rng, count)
    heavy_load, common = load_shares(count, rows * top, most, lean, True), load_shares(count, rows * top, most, lean, False)
    places = jnp.arange(count)

    def named(tallies, turn):
        used = int((tallies > 0).sum())
        fixed = max(1, used // 4)
        shifted = fixed + (places - fixed + turn * (used - fixed)) % max(1, count - fixed)
        return jnp.zeros((count,), jnp.int32).at[ranking[jnp.where(places < fixed, places, shifted)]].set(jnp.asarray(tallies, jnp.int32))

    tallies = jnp.where(number % 4 == 0, named(heavy_load, number // 4), named(common, number - number // 4 - 1))
    mixed = jax.random.permutation(jax.random.fold_in(own, 3), count)
    giver, receiver = mixed[0:count // 2 * 2:2], mixed[1:count // 2 * 2:2]
    room = jnp.minimum(tallies[giver] - 1, most - tallies[receiver]) // 2
    room = jnp.where((giver == ranking[0]) | (receiver == ranking[0]) | (tallies[receiver] == 0), 0, jnp.maximum(room, 0))
    shifted = jax.random.randint(jax.random.fold_in(own, 4), (count // 2,), 0, 1 << 20) % (room + 1)
    tallies = tallies.at[giver].add(-shifted).at[receiver].add(shifted)
    members = jnp.searchsorted(jnp.cumsum(tallies), jnp.arange(rows * top), side="right").astype(jnp.int32)
    listing = members.reshape(top, rows).T
    listing = listing[jax.random.permutation(jax.random.fold_in(own, 1), rows)]
    turn = jax.random.randint(jax.random.fold_in(own, 2), (rows, 1), 0, top)
    return jnp.take_along_axis(listing, (jnp.arange(top)[None, :] + turn) % top, axis=1)


def load_shares(number_of, total, limit, slope, full):
    portions = [(1 << 20) // math.isqrt(standing ** slope) + 1 for standing in range(1, number_of + 1)]
    largest = limit if full else min(limit, max(-(-total // number_of), total * portions[0] // sum(portions)))
    least = 1 if total - largest >= number_of - 1 else 0
    given, rest = [largest] + [least] * (number_of - 1), total - largest - least * (number_of - 1)
    while rest > 0:
        free = [i for i in range(1, number_of) if given[i] < largest] or [i for i in range(1, number_of) if given[i] < limit]
        mass, left = sum([portions[i] for i in free]), rest
        for i in free:
            more = min(limit - given[i], max(1, left * portions[i] // mass), rest)
            given[i] = given[i] + more
            rest = rest - more
    return np.array(given)


def scatter_about(key, dims, width, reach, shards=(), held_as=jnp.bfloat16):
    drawn = jax.random.normal(key, dims, jnp.float32) * width
    if len(shards) > 0:
        drawn = block_scale(key, dims, shards, -0.22, 0.18) * drawn
    return jnp.clip(drawn, min=-reach, max=reach).astype(held_as)


def setup_inputs(seed: int = 0) -> dict:
    streams_of = jax.random.split(jax.random.key(seed), 12)
    queries = draw_queries(jax.random.fold_in(streams_of[11], 71), 0)
    memory_keys = draw_memory_keys(jax.random.fold_in(streams_of[11], 71), 0)
    memory_values = scatter_about(streams_of[2], (BATCH, LMEM, D), 1.0, 6.0, ((0, 8), (1, 16)))
    stream = draw_stream(jax.random.fold_in(streams_of[11], 71), 0)
    norm_gain = jnp.clip(1.0 + 0.18 * jax.random.normal(streams_of[4], (D,), jnp.float32), 0.1, 1.9)
    gate_proj = scatter_about(streams_of[5], (EXPERTS, D, FF), D ** -0.5, 0.1875, ((0, 16), (2, 8)))
    up_proj = scatter_about(streams_of[6], (EXPERTS, D, FF), D ** -0.5, 0.1875, ((0, 16), (2, 8)))
    down_proj = scatter_about(streams_of[7], (EXPERTS, FF, D), FF ** -0.5, 0.109375, ((0, 16), (1, 8)))
    expert_ids_keys = jax.random.split(jax.random.fold_in(streams_of[8], 1), N_SEQ * GROUPS * TOK_DEV // TOK_DEV)
    expert_ids_turns = jax.random.permutation(jax.random.fold_in(streams_of[8], 3), N_SEQ * GROUPS * TOK_DEV // TOK_DEV)
    expert_ids = jax.vmap(lambda own, number: assign_block(jax.random.fold_in(streams_of[8], 2), own, number, TOK_DEV, EXPERTS, 2, CAP, 2))(expert_ids_keys, expert_ids_turns).reshape((N_SEQ, GROUPS, TOK_DEV, 2))
    gate_weights = jnp.clip(0.099609375 + 0.7988281 * jax.random.uniform(streams_of[9], (N_SEQ, GROUPS, TOK_DEV, 2), jnp.float32) ** block_scale(streams_of[9], (N_SEQ, GROUPS, TOK_DEV, 2), ((0, 16), (1, 8)), -0.2, 0.2), 0.099609375, 0.8984375).astype(jnp.bfloat16)
    upstream_grad = scatter_about(streams_of[10], (BATCH, LDEC, D), 1.0, 6.0, ((0, 8), (1, 16)))
    return dict(queries=queries, memory_keys=memory_keys, memory_values=memory_values, stream=stream, norm_gain=norm_gain, gate_proj=gate_proj, up_proj=up_proj, down_proj=down_proj, expert_ids=expert_ids, gate_weights=gate_weights, upstream_grad=upstream_grad)


EPSILON = 1e-06

def gelu_pair(preact):
    normal_cdf = 0.5 * (1.0 + lax.erf(preact * 0.7071067811865476))
    normal_pdf = jnp.exp(-0.5 * preact * preact) * 0.3989422804014327
    return (preact * normal_cdf, normal_cdf + preact * normal_pdf)

def rounded_result(values_in):
    return lax.optimization_barrier(values_in.astype(jnp.bfloat16)).astype(jnp.float32)

def to_device_order(tensor_in):
    groups = N_EXPERT * N_DP
    trailing = tensor_in.shape[2:]
    tensor_in = tensor_in.reshape((groups, EX_DEV, N_SEQ, DEC_DEV) + trailing)
    tensor_in = jnp.swapaxes(jnp.swapaxes(tensor_in, 1, 2), 0, 1)
    return tensor_in.reshape((N_SEQ * groups, EX_DEV * DEC_DEV) + trailing)

def to_batch_order(tensor_in):
    groups = N_EXPERT * N_DP
    trailing = tensor_in.shape[2:]
    tensor_in = tensor_in.reshape((N_SEQ, groups, EX_DEV, DEC_DEV) + trailing)
    tensor_in = jnp.swapaxes(jnp.swapaxes(tensor_in, 0, 1), 1, 2)
    return tensor_in.reshape((BATCH, LDEC) + trailing)

def expert_grads(operands):
    inputs, cotangent, gates_in, gate_w, up_w, down_w = operands
    pre_gate = jnp.dot(inputs, gate_w, preferred_element_type=jnp.float32)
    pre_up = jnp.dot(inputs, up_w, preferred_element_type=jnp.float32)
    activated, gelu_slope = gelu_pair(pre_gate)
    hidden = (activated * pre_up).astype(jnp.bfloat16)
    cot_float = cotangent.astype(jnp.float32)
    out_rows = jnp.dot(hidden, down_w, preferred_element_type=jnp.float32)
    gate_terms = lax.optimization_barrier(jnp.sum(out_rows * cot_float, axis=-1))
    scaled = (cot_float * gates_in.astype(jnp.float32)[:, None]).astype(jnp.bfloat16)
    d_hidden = jnp.dot(scaled, down_w.T, preferred_element_type=jnp.float32)
    d_pre_gate = (d_hidden * pre_up * gelu_slope).astype(jnp.bfloat16)
    d_pre_up = (d_hidden * activated).astype(jnp.bfloat16)
    d_inputs = jnp.dot(d_pre_gate, gate_w.T, preferred_element_type=jnp.float32) + jnp.dot(d_pre_up, up_w.T, preferred_element_type=jnp.float32)
    grad_gate = jnp.dot(inputs.T, d_pre_gate, preferred_element_type=jnp.float32).astype(jnp.bfloat16)
    grad_up = jnp.dot(inputs.T, d_pre_up, preferred_element_type=jnp.float32).astype(jnp.bfloat16)
    grad_down = jnp.dot(hidden.T, scaled, preferred_element_type=jnp.float32).astype(jnp.bfloat16)
    return (d_inputs, gate_terms, grad_gate, grad_up, grad_down)

def reference(queries, memory_keys, memory_values, stream, norm_gain, gate_proj, up_proj, down_proj, expert_ids, gate_weights, upstream_grad):
    devices_all = N_SEQ * N_EXPERT * N_DP
    stream_rows = to_device_order(stream).astype(jnp.float32)
    inverse = lax.rsqrt(lax.optimization_barrier(jnp.mean(stream_rows * stream_rows, axis=-1, keepdims=True)) + EPSILON)
    unit_rows = stream_rows * inverse
    normed = (unit_rows * norm_gain).astype(jnp.bfloat16)
    cot_rows = to_device_order(upstream_grad)
    picks = expert_ids.reshape(devices_all, 2 * TOK_DEV).astype(jnp.int32)
    one_hot = (picks[:, :, None] == jnp.arange(EXPERTS, dtype=jnp.int32)[None, None, :]).astype(jnp.int32)
    earlier = (jnp.cumsum(one_hot, axis=1) - one_hot).astype(jnp.int32)
    slot_index = lax.optimization_barrier(jnp.sum(earlier * one_hot, axis=2)).astype(jnp.int32)
    row_index = (jnp.arange(devices_all, dtype=jnp.int32)[:, None] * CAP + slot_index).astype(jnp.int32)
    buffer_rows = jnp.zeros((EXPERTS, devices_all * CAP, D), jnp.bfloat16).at[picks, row_index].set(jnp.repeat(normed, 2, axis=1))
    buffer_cots = jnp.zeros((EXPERTS, devices_all * CAP, D), jnp.bfloat16).at[picks, row_index].set(jnp.repeat(cot_rows, 2, axis=1))
    buffer_gates = jnp.zeros((EXPERTS, devices_all * CAP), jnp.bfloat16).at[picks, row_index].set(gate_weights.reshape(devices_all, 2 * TOK_DEV))
    d_inputs, gate_terms, gate_proj_grad, up_proj_grad, down_proj_grad = lax.map(expert_grads, (buffer_rows, buffer_cots, buffer_gates, gate_proj, up_proj, down_proj))
    pair_rows = d_inputs[picks, row_index]
    d_normed = lax.optimization_barrier(jnp.sum(pair_rows.reshape(devices_all, TOK_DEV, 2, D), axis=2))
    gate_weights_grad = gate_terms[picks, row_index].reshape(expert_ids.shape)
    gain_grad = lax.optimization_barrier(jnp.sum(d_normed * unit_rows, axis=(0, 1)))
    scaled_grad = d_normed * norm_gain
    stream_rows_grad = cot_rows.astype(jnp.float32) + inverse * (scaled_grad - unit_rows * lax.optimization_barrier(jnp.mean(scaled_grad * unit_rows, axis=-1, keepdims=True)))
    stream_grad = to_batch_order(stream_rows_grad.astype(jnp.bfloat16))
    logit_scale = float(HD) ** (-0.5)

    def one_example(operands):
        query_ex, key_ex, value_ex, grad_ex = operands
        query_head_rows = query_ex.astype(jnp.float32).reshape(LDEC, HEADS, HD)
        key_head_rows = key_ex.astype(jnp.float32).reshape(LMEM, HEADS, HD)
        value_head_rows = value_ex.astype(jnp.float32).reshape(LMEM, HEADS, HD)
        head_gradients = grad_ex.astype(jnp.float32).reshape(LDEC, HEADS, HD)
        attention_logits = jnp.einsum('eyi,kyi->yek', query_head_rows, key_head_rows) * logit_scale
        row_peak = lax.optimization_barrier(jnp.max(attention_logits, axis=-1, keepdims=True))
        log_total = row_peak + jnp.log(lax.optimization_barrier(jnp.sum(jnp.exp(attention_logits - row_peak), axis=-1, keepdims=True)))
        softmax_weights = jnp.exp(attention_logits - log_total)
        value_portion = jnp.einsum('iun,uic->nic', rounded_result(softmax_weights), head_gradients)
        probability_gradient = jnp.einsum('eyi,kyi->yek', head_gradients, value_head_rows)
        delta_sum = lax.optimization_barrier(jnp.sum(softmax_weights * probability_gradient, axis=-1, keepdims=True))
        score_gradient = rounded_result(softmax_weights * (probability_gradient - delta_sum))
        key_portion = jnp.einsum('iun,uic->nic', score_gradient, query_head_rows) * logit_scale
        query_portion = jnp.einsum('cso,oca->sca', score_gradient, key_head_rows) * logit_scale
        return (query_portion.reshape(LDEC, D).astype(jnp.bfloat16), key_portion.reshape(LMEM, D).astype(jnp.bfloat16), value_portion.reshape(LMEM, D).astype(jnp.bfloat16))
    queries_grad, keys_grad, values_grad = lax.map(one_example, (queries, memory_keys, memory_values, stream_grad))
    return (queries_grad, keys_grad, values_grad, stream_grad, gain_grad, gate_proj_grad, up_proj_grad, down_proj_grad, gate_weights_grad)
```

```python
import functools

import jax
import jax.numpy as jnp
import numpy as np
from jax import lax
from jax.experimental import pallas as pl
from jax.experimental.pallas import tpu as pltpu
from jax.sharding import PartitionSpec as P

HEADS = 16
EPSILON = 1e-06
CAP = 12
BACK = 16
GROUP = 8
F32 = jnp.float32
BF16 = jnp.bfloat16
HBM = pl.BlockSpec(memory_space=pltpu.HBM)


def lasts(us):
    return pl.CostEstimate(flops=1, bytes_accessed=int(us * 3.2e6), transcendentals=0)


def dot(a, b, ca=1, cb=0):
    return lax.dot_general(a, b, (((ca,), (cb,)), ((), ())), preferred_element_type=F32)


def xor_swap(value, axis, bits):
    size = lax.axis_size(axis)
    return lax.ppermute(value, axis, [(i, i ^ bits) for i in range(size)])


def shift(value, axis, by):
    size = lax.axis_size(axis)
    return lax.ppermute(value, axis, [(i, (i + by) % size) for i in range(size)])


def on_chip(kernel, out_shape, args, *, us, after=(), vmem=16, scratch=(), far_in=(), far_out=()):
    count = len(args)
    near = pl.BlockSpec(memory_space=pltpu.VMEM)
    outs = out_shape if isinstance(out_shape, list) else [out_shape]
    outs = [pltpu.HBM(o.shape, o.dtype) if i in far_out else o for i, o in enumerate(outs)]
    args = [stay(a) if i in far_in else a for i, a in enumerate(args)]

    def body(*refs):
        kernel(*refs[:count], *refs[count + len(after) :])

    result = pl.pallas_call(
        body,
        out_shape=outs,
        in_specs=[HBM if i in far_in else near for i in range(count)]
        + [pl.BlockSpec(memory_space=pl.ANY)] * len(after),
        out_specs=[HBM if i in far_out else near for i in range(len(outs))],
        scratch_shapes=list(scratch),
        compiler_params=pltpu.CompilerParams(vmem_limit_bytes=vmem << 20),
        cost_estimate=lasts(us),
    )(*args, *after)
    return result if isinstance(out_shape, list) else result[0]


def stay(array):
    return pltpu.with_memory_space_constraint(array, pltpu.HBM)


def sds(shape, dtype=BF16):
    return jax.ShapeDtypeStruct(shape, dtype)


def iota(shape, dim):
    return lax.broadcasted_iota(jnp.int32, shape, dim)


def mask(cond):
    return jnp.where(cond, 1.0, 0.0).astype(BF16)


def dispatch_kernel(experts, x_ref, gain_ref, cot_ref, idt_ref, gt_ref, send_ref):
    tokens = x_ref.shape[0]
    x = x_ref[...].astype(F32)
    inverse = lax.rsqrt(jnp.mean(x * x, axis=-1, keepdims=True) + EPSILON)
    normed = (x * inverse * gain_ref[...]).astype(BF16)
    e_of = iota((experts, tokens), 0)
    hot = [idt_ref[k : k + 1, :] == e_of for k in range(2)]
    before = mask(iota((tokens, tokens), 0) < iota((tokens, tokens), 1))
    count = dot(mask(hot[0] | hot[1]), before)
    rows = experts * 2 * CAP
    r_of = iota((rows, tokens), 0)
    plain, weighted = None, 0.0
    for k in range(2):
        slot = jnp.sum(jnp.where(hot[k], count, 0.0), axis=0, keepdims=True)
        at = idt_ref[k : k + 1, :] * (2 * CAP) + slot.astype(jnp.int32)
        here = r_of == at
        plain = here if plain is None else plain | here
        g = gt_ref[k : k + 1, :].astype(F32)
        weighted = weighted + jnp.where(r_of == at + CAP, g, 0.0)
    choose = jnp.concatenate([mask(plain), weighted.astype(BF16)], axis=1)
    sources = jnp.concatenate([normed, cot_ref[...]], axis=0)
    send_ref[...] = dot(choose, sources).astype(BF16)


def pick(at, weights, after, us):
    _, hid, width = weights[0].shape
    count = len(weights)

    def body(at_ref, *refs):
        out_ref, sems = refs[-2:]
        copies = [
            pltpu.make_async_copy(ref.at[at_ref[0]], out_ref.at[kind], sems.at[kind])
            for kind, ref in enumerate(refs[:count])
        ]
        for copy in copies:
            copy.start()
        for copy in copies:
            copy.wait()

    return pl.pallas_call(
        body,
        in_specs=[pl.BlockSpec(memory_space=pltpu.SMEM)]
        + [HBM] * count
        + [pl.BlockSpec(memory_space=pl.ANY)] * len(after),
        out_specs=pl.BlockSpec(memory_space=pltpu.VMEM),
        out_shape=sds((count, hid, width)),
        scratch_shapes=[pltpu.SemaphoreType.DMA((count,))],
        compiler_params=pltpu.CompilerParams(vmem_limit_bytes=16 << 20),
        cost_estimate=lasts(us),
    )(at, *[stay(w) for w in weights], *after)


def place(at, mine, got, after):
    kinds = len(mine)
    hid, width = mine[0].shape

    def body(at_ref, *refs):
        mine_refs, got_refs = refs[:kinds], refs[kinds : 2 * kinds]
        outs, sems = refs[2 * kinds + len(after) : -1], refs[-1]
        at = at_ref[0]
        copies = []
        for k, out in enumerate(outs):
            for j, (src, there) in enumerate(((mine_refs[k], at), (got_refs[k], 1 - at))):
                copies.append(pltpu.make_async_copy(src, out.at[there], sems.at[2 * k + j]))
        for copy in copies:
            copy.start()
        for copy in copies:
            copy.wait()

    return pl.pallas_call(
        body,
        out_shape=[pltpu.HBM((2, hid, width), BF16)] * kinds,
        in_specs=[pl.BlockSpec(memory_space=pltpu.SMEM)]
        + [pl.BlockSpec(memory_space=pltpu.VMEM)] * (2 * kinds)
        + [pl.BlockSpec(memory_space=pl.ANY)] * len(after),
        out_specs=[HBM] * kinds,
        scratch_shapes=[pltpu.SemaphoreType.DMA((2 * kinds,))],
        compiler_params=pltpu.CompilerParams(vmem_limit_bytes=16 << 20),
        cost_estimate=lasts(3),
    )(at, *mine, *got, *after)


def separate(sx_ref, ss_ref, part_ref, xs_ref, j):
    step = GROUP * CAP
    for i in range(part_ref.shape[0] // (2 * step)):
        block = part_ref[2 * step * i : 2 * step * (i + 1), :]
        at = slice(step * j, step * (j + 1))
        xs_ref[0, at, :] = dot(sx_ref[...], block).astype(BF16)
        xs_ref[1, at, :] = dot(ss_ref[...], block).astype(BF16)
        j += 1
    return j


def hidden_block(xs_ref, w_ref, saved_ref):
    pre_gate = dot(xs_ref[0], w_ref[0], 1, 1)
    pre_up = dot(xs_ref[0], w_ref[1], 1, 1)
    d_hidden = dot(xs_ref[1], w_ref[2], 1, 1)
    cdf = 0.5 * (1.0 + lax.erf(pre_gate * 0.7071067811865476))
    pdf = jnp.exp(-0.5 * pre_gate * pre_gate) * 0.3989422804014327
    activated = pre_gate * cdf
    hidden = (activated * pre_up).astype(BF16)
    d_gate = (d_hidden * pre_up * (cdf + pre_gate * pdf)).astype(BF16)
    d_up = (d_hidden * activated).astype(BF16)
    for kind, value in enumerate((d_gate, d_up, hidden)):
        saved_ref[kind] = value
    rows = dot(d_gate, w_ref[0]) + dot(d_up, w_ref[1])
    return rows, jnp.sum(hidden.astype(F32) * d_hidden, axis=1, keepdims=True)


def put_back(back_ref, total, gate):
    rows = total.shape[0]
    back_ref[:rows, :] = total.astype(BF16)
    spread = jnp.broadcast_to(gate, (rows, 128)).T
    back_ref[rows:, :rows] = spread[:16, :].astype(BF16)
    back_ref[rows:, rows:] = jnp.zeros((16, back_ref.shape[1] - rows), BF16)


def piece_kernel(count, sx_ref, ss_ref, *refs):
    parts, refs = refs[:count], refs[count:]
    blocks = (len(refs) - 6) // 2
    weights, refs = refs[:blocks], refs[blocks:]
    back_ref, xs_out, refs = refs[0], refs[1], refs[2:]
    saved_outs, (part_scr, xs_ref, saved_ref), sems = refs[:blocks], refs[blocks:-1], refs[-1]
    size = parts[0].shape[0]
    fetches = [
        pltpu.make_async_copy(p, part_scr.at[pl.ds(size * i, size), :], sems.at[i])
        for i, p in enumerate(parts)
    ]
    for fetch in fetches:
        fetch.start()
    j = 0
    for i, fetch in enumerate(fetches):
        fetch.wait()
        j = separate(sx_ref, ss_ref, part_scr.at[pl.ds(size * i, size), :], xs_ref, j)
    stores = [pltpu.make_async_copy(xs_ref, xs_out, sems.at[count])]
    stores[0].start()
    total, gate = None, None
    for n, w_ref in enumerate(weights):
        rows, terms = hidden_block(xs_ref, w_ref, saved_ref.at[n])
        stores.append(
            pltpu.make_async_copy(saved_ref.at[n], saved_outs[n], sems.at[count + 1 + n])
        )
        stores[-1].start()
        total = rows if n == 0 else total + rows
        gate = terms if n == 0 else gate + terms
    put_back(back_ref, total, gate)
    for store in stores:
        store.wait()


def second_half_kernel(xs_in, w_ref, part_ref, back_ref, saved_out, xs_ref, saved_ref, sems):
    fetch = pltpu.make_async_copy(xs_in, xs_ref, sems.at[0])
    fetch.start()
    fetch.wait()
    total, gate = hidden_block(xs_ref, w_ref, saved_ref)
    store = pltpu.make_async_copy(saved_ref, saved_out, sems.at[1])
    store.start()
    put_back(back_ref, total, gate)
    back_ref[...] = (back_ref[...].astype(F32) + part_ref[...].astype(F32)).astype(BF16)
    store.wait()


def expert_piece(parts, weights, sel, after):
    width = parts[0].shape[-1]
    parts = [p.reshape(-1, width) for p in parts]
    rows = sum(p.shape[0] for p in parts) // 2
    hid = weights[0].shape[1]
    blocks, count = len(weights), len(parts)
    return on_chip(
        functools.partial(piece_kernel, count),
        [sds((rows + 16, width)), sds((2, rows, width))] + [sds((3, rows, hid))] * blocks,
        [*sel, *parts, *weights],
        us=0.5,
        vmem=24,
        after=after,
        scratch=[
            pltpu.VMEM((2 * rows, width), BF16),
            pltpu.VMEM((2, rows, width), BF16),
            pltpu.VMEM((blocks, 3, rows, hid), BF16),
            pltpu.SemaphoreType.DMA((count + 1 + blocks,)),
        ],
        far_in=range(2, 2 + count),
        far_out=range(1, 2 + blocks),
    )


def second_half(xs, got_w, part, after):
    saved = (3, xs.shape[1], got_w.shape[1])
    return on_chip(
        second_half_kernel,
        [sds(part.shape), sds(saved)],
        [xs, got_w, part],
        us=0.5,
        after=after,
        scratch=[
            pltpu.VMEM(xs.shape, BF16),
            pltpu.VMEM(saved, BF16),
            pltpu.SemaphoreType.DMA((2,)),
        ],
        far_in=(0,),
        far_out=(1,),
    )


def weight_kernel(n, *refs):
    ins, outs = refs[: 2 * n], refs[2 * n : 2 * n + 3]
    xs_ref, saved_ref, acc_ref, sems = refs[2 * n + 3 :]
    fetches = []
    for z in range(n):
        for i, ref in enumerate((xs_ref, saved_ref)):
            fetches.append(pltpu.make_async_copy(ins[2 * z + i], ref.at[z], sems.at[2 * z + i]))
            fetches[-1].start()
    for z in range(n):
        fetches[2 * z].wait()
        fetches[2 * z + 1].wait()
        for kind, out_ref in enumerate(outs):
            part = dot(saved_ref[z, kind], xs_ref[z, kind // 2], 0, 0)
            if z > 0:
                part = part + acc_ref[kind]
            if z == n - 1:
                out_ref[...] = part.astype(BF16)
            else:
                acc_ref[kind] = part


def weight_grads(results, half, after):
    xs, saved = results[0][1:3]
    n, (_, rows, hid), width = len(results), saved.shape, xs.shape[2]
    return on_chip(
        functools.partial(weight_kernel, n),
        [sds((hid, width))] * 3,
        [a for r in results for a in (r[1], r[2 + half])],
        us=0.5,
        vmem=28,
        after=after,
        scratch=[
            pltpu.VMEM((n, 2, rows, width), BF16),
            pltpu.VMEM((n, 3, rows, hid), BF16),
            pltpu.VMEM((3, hid, width), F32),
            pltpu.SemaphoreType.DMA((2 * n,)),
        ],
        far_in=range(2 * n),
    )


def payload_kernel(spread_ref, ga_ref, gb_ref, xs_ref, a_ref, b_ref, c_ref, d_ref, out_ref):
    rows = a_ref.shape[0] - 16
    step = GROUP * CAP
    total = (a_ref[...].astype(F32) + b_ref[...].astype(F32)) + (
        c_ref[...].astype(F32) + d_ref[...].astype(F32)
    )
    gates = total[rows : rows + 1, :rows]
    total = total[:rows, :]
    gain = jnp.sum(total * xs_ref[0].astype(F32), axis=0, keepdims=True)
    coarse = gain.astype(BF16)
    fine = (gain - coarse.astype(F32)).astype(BF16)
    order = iota((16, gain.shape[1]), 0)
    gains = jnp.where(order == 0, coarse.astype(F32), 0.0) + jnp.where(
        order == 1, fine.astype(F32), 0.0
    )
    gains = gains.astype(BF16)
    total = total.astype(BF16)
    wide = GROUP * BACK
    for j in range(rows // step):
        block = jnp.concatenate([total[step * j : step * (j + 1), :], gains], axis=0)
        out_ref[wide * j : wide * (j + 1), :] = dot(spread_ref[...], block).astype(BF16)
    placed = dot((ga_ref[...].astype(F32) * gates).astype(BF16), gb_ref[...]).astype(BF16)
    out_ref[:, :128] = out_ref[:, :128] + placed


def column(row):
    count = row.shape[1]
    return jnp.broadcast_to(row, (count, count)).T[:, :1]


def combine_kernel(
    experts, r_ref, x_ref, gain_ref, cot_ref, idt_ref, gt_ref, out_ref, heads_ref, gain_out, gates_out
):
    tokens = x_ref.shape[0]
    e_of = iota((tokens, experts), 1)
    ids = [column(idt_ref[k : k + 1, :].astype(F32)).astype(jnp.int32) for k in range(2)]
    hot = [i == e_of for i in ids]
    before = mask(iota((tokens, tokens), 1) < iota((tokens, tokens), 0))
    count = dot(before, mask(hot[0] | hot[1]))
    slots = [
        jnp.sum(jnp.where(h, count, 0.0), axis=1, keepdims=True).astype(jnp.int32) for h in hot
    ]
    r_of = iota((tokens, experts * BACK), 1)
    take = mask((r_of == ids[0] * BACK + slots[0]) | (r_of == ids[1] * BACK + slots[1]))
    d_normed = dot(take, r_ref[...])
    lane = iota((tokens, 128), 1)
    for k in range(2):
        line = dot(mask(r_of == ids[k] * BACK + CAP), r_ref[:, :128])
        found = jnp.sum(jnp.where(lane == slots[k], line, 0.0), axis=1, keepdims=True)
        gates_out[:, k : k + 1] = found / column(gt_ref[k : k + 1, :].astype(F32))
    gain = gain_ref[...]
    line_of = iota((16, experts * BACK), 1) % BACK
    sums = dot(mask((line_of == CAP + 1) | (line_of == CAP + 2)), r_ref[...])
    gain_out[...] = sums[:1, :] / gain
    x = x_ref[...].astype(F32)
    inverse = lax.rsqrt(jnp.mean(x * x, axis=-1, keepdims=True) + EPSILON)
    unit = x * inverse
    scaled = d_normed * gain
    grad = cot_ref[...].astype(F32) + inverse * (
        scaled - unit * jnp.mean(scaled * unit, axis=-1, keepdims=True)
    )
    grad = grad.astype(BF16)
    out_ref[...] = grad
    put_heads(heads_ref, 0, grad)


def put_heads(out_ref, offset, rows):
    half = rows.shape[0] // 2
    count = rows.shape[1] // 128
    for pair in range(2):
        for head in range(count):
            out_ref[pair * count + head, offset : offset + half, :] = rows[
                pair * half : (pair + 1) * half, head * 128 : (head + 1) * 128
            ]


def pack_kernel(q_ref, k_ref, v_ref, out_ref):
    offset = 0
    for ref in (q_ref, k_ref, v_ref):
        put_heads(out_ref, offset, ref)
        offset += ref.shape[0] // 2


def unpack_kernel(in_ref, *outs):
    offset = 0
    for ref in outs:
        half = ref.shape[0] // 2
        count = ref.shape[1] // 128
        for pair in range(2):
            for head in range(count):
                ref[pair * half : (pair + 1) * half, head * 128 : (head + 1) * 128] = in_ref[
                    pair * count + head, offset : offset + half, :
                ]
        offset += half


def cut_kernel(prev_ref, next_ref, low_ref, high_ref):
    half = low_ref.shape[0]
    low_ref[...] = prev_ref[:half]
    high_ref[...] = next_ref[half:]


def attn_forward_kernel(n_q, n_m, scale, b, qkv_ref, p_out, o_ref, s_scr, p_ref, sems):
    seq = qkv_ref.shape[0]
    lq = seq * n_q
    per = 2
    chunk = per * n_m
    count = seq // per
    q = qkv_ref[:, pl.ds(b * n_q, n_q), :].reshape(lq, 128)
    qt = (q.astype(F32) * scale).T
    half_of = iota((128, lq), 0) < 64
    k_at = 2 * n_q + b * n_m
    v_at = 2 * n_q + 2 * n_m + b * n_m
    for h in range(2):
        qh = jnp.where(half_of if h == 0 else jnp.logical_not(half_of), qt, 0.0).astype(BF16)

        def score(c, peak):
            k = qkv_ref[pl.ds(c * per, per), pl.ds(k_at, n_m), :].reshape(chunk, 128)
            s = dot(k, qh)
            s_scr[pl.ds(pl.multiple_of(c * chunk, chunk), chunk), :] = s
            return jnp.maximum(peak, jnp.max(s, axis=0, keepdims=True))

        peak = lax.fori_loop(0, count, score, jnp.full((1, lq), -jnp.inf, F32))

        def power(c, total):
            at = pl.ds(pl.multiple_of(c * chunk, chunk), chunk)
            e = jnp.exp(s_scr[at, :] - peak)
            s_scr[at, :] = e
            return total + jnp.sum(e, axis=0, keepdims=True)

        total = lax.fori_loop(0, count, power, jnp.zeros((1, lq), F32))
        factor = 1.0 / total

        def finish(c, out):
            at = pl.ds(pl.multiple_of(c * chunk, chunk), chunk)
            p = (s_scr[at, :] * factor).astype(BF16)
            p_ref[h, at, :] = p
            v = qkv_ref[pl.ds(c * per, per), pl.ds(v_at, n_m), :].reshape(chunk, 128)
            vt = v.astype(F32).T.astype(BF16)
            return out + dot(vt[64 * h : 64 * h + 64, :], p)

        o_ref[64 * h : 64 * h + 64, :] = lax.fori_loop(
            0, count, finish, jnp.zeros((64, lq), F32)
        )
        pltpu.make_async_copy(p_ref.at[h], p_out.at[h], sems.at[h]).start()
    for h in range(2):
        pltpu.make_async_copy(p_ref.at[h], p_out.at[h], sems.at[h]).wait()


def attn_backward_kernel(
    n_q, n_m, scale, qkv_ref, do_ref, p0_ref, p1_ref, o0_ref, o1_ref, out_ref, dq_scr, p_scr, sems
):
    seq = qkv_ref.shape[0]
    lq = seq * n_q
    per = 4
    chunk = per * n_m
    lane = iota((lq, 128), 1) < 64
    row = iota((128, lq), 0) < 64
    zero = jnp.zeros((), BF16)
    p_refs = (p0_ref, p1_ref)

    def fetch(b, c):
        at = pl.ds(c * chunk, chunk)
        return pltpu.make_async_copy(p_refs[b].at[:, at, :], p_scr.at[b, :, at, :], sems.at[b, c])

    for b in range(2):
        for c in range(seq // per):
            fetch(b, c).start()
    for b, o_ref in enumerate((o0_ref, o1_ref)):
        q_at = pl.ds(b * n_q, n_q)
        k_at = pl.ds(2 * n_q + b * n_m, n_m)
        v_at = pl.ds(2 * n_q + 2 * n_m + b * n_m, n_m)
        d_out = do_ref[:, q_at, :].reshape(lq, 128)
        dt = d_out.astype(F32).T
        prod = dt * o_ref[...]
        delta = [jnp.sum(prod[64 * h : 64 * h + 64, :], axis=0, keepdims=True) for h in range(2)]
        dt = dt.astype(BF16)
        q = (qkv_ref[:, q_at, :].reshape(lq, 128).astype(F32) * scale).astype(BF16)
        rows_of = [jnp.where(row, dt, zero), jnp.where(row, zero, dt)]
        d_out_of = [jnp.where(lane, d_out, zero), jnp.where(lane, zero, d_out)]
        q_of = [jnp.where(lane, q, zero), jnp.where(lane, zero, q)]
        dq_scr[...] = jnp.zeros_like(dq_scr)

        for c in range(seq // per):
            src = pl.ds(c * per, per)
            at = pl.ds(c * chunk, chunk)
            fetch(b, c).wait()
            k = qkv_ref[src, k_at, :].reshape(chunk, 128)
            v = qkv_ref[src, v_at, :].reshape(chunk, 128)
            kt = k.astype(F32).T.astype(BF16)
            dk, dv = None, None
            for h in range(2):
                d_p = dot(v, rows_of[h])
                p = p_scr[b, h, at, :]
                ds = (p.astype(F32) * (d_p - delta[h])).astype(BF16)
                dv_h = dot(p, d_out_of[h])
                dk_h = dot(ds, q_of[h])
                dv = dv_h if dv is None else dv + dv_h
                dk = dk_h if dk is None else dk + dk_h
                mine = slice(64 * h, 64 * h + 64)
                dq_scr[mine, :] += dot(kt[mine, :], ds)
            out_ref[src, k_at, :] = dk.astype(BF16).reshape(per, n_m, 128)
            out_ref[src, v_at, :] = dv.astype(BF16).reshape(per, n_m, 128)
        dq = (dq_scr[...] * scale).T.astype(BF16)
        out_ref[:, q_at, :] = dq.reshape(seq, n_q, 128)


def attn_forward(qkv, example, n_q, n_m, scale, after):
    seq = qkv.shape[0]
    lq, lm = seq * n_q, seq * n_m
    return on_chip(
        functools.partial(attn_forward_kernel, n_q, n_m, scale, example),
        [sds((2, lm, lq)), sds((128, lq), F32)],
        [qkv],
        us=8.7,
        after=after,
        scratch=[
            pltpu.VMEM((lm, lq), F32),
            pltpu.VMEM((2, lm, lq), BF16),
            pltpu.SemaphoreType.DMA((2,)),
        ],
        far_out=(0,),
    )


def attn_backward(qkv, d_out, probs, o_t, n_q, n_m, scale, after):
    seq = qkv.shape[0]
    lq = seq * n_q
    return on_chip(
        functools.partial(attn_backward_kernel, n_q, n_m, scale),
        sds(qkv.shape),
        [qkv, d_out, *probs, *o_t],
        us=11,
        after=after,
        vmem=24,
        scratch=[
            pltpu.VMEM((128, lq), F32),
            pltpu.VMEM((2, 2, seq * n_m, lq), BF16),
            pltpu.SemaphoreType.DMA((2, seq // 4)),
        ],
        far_in=(2, 3),
    )


def selections(experts):
    r = np.arange(GROUP * CAP)
    c = np.arange(2 * GROUP * CAP)
    first = c[None, :] == ((r // CAP) * 2 * CAP + r % CAP)[:, None]
    second = c[None, :] == ((r // CAP) * 2 * CAP + r % CAP + CAP)[:, None]
    o = np.arange(GROUP * BACK)
    spread = (r[None, :] == ((o // BACK) * CAP + o % BACK)[:, None]) & (o % BACK < CAP)[:, None]
    extra = (o % BACK)[:, None] == (CAP + 1 + np.arange(16))[None, :]
    spread = np.concatenate([spread, extra], axis=1)
    o_all = np.arange(experts * BACK)
    c_all = np.arange(experts * CAP)
    lines = (o_all % BACK == CAP)[:, None] & (c_all[None, :] // CAP == o_all[:, None] // BACK)
    lanes = c_all[:, None] % CAP == np.arange(128)[None, :]
    return [jnp.asarray(m.astype(np.float32), BF16) for m in (first, second, spread, lines, lanes)]


def on_device(
    queries,
    memory_keys,
    memory_values,
    stream,
    norm_gain,
    gate_proj,
    up_proj,
    down_proj,
    expert_ids,
    gate_weights,
    upstream_grad,
):
    examples, positions, width = stream.shape
    mem_rows = memory_keys.shape[1]
    tokens = examples * positions
    experts = lax.axis_size("seq") * gate_proj.shape[0]
    logit_scale = (width // HEADS) ** (-0.5)
    my_dp = lax.axis_index("dp")
    sel_x, sel_s, spread, lines, lanes = selections(experts)

    w_t = [jnp.swapaxes(gate_proj, 1, 2), jnp.swapaxes(up_proj, 1, 2), down_proj]
    hid = w_t[2].shape[1]
    at = my_dp.reshape(1).astype(jnp.int32)
    give_w = pick(1 - at, w_t, [], 1)
    got_w = xor_swap(give_w, "dp", 1)

    x_rows = stream.reshape(tokens, width)
    cot_rows = upstream_grad.reshape(tokens, width)
    gain_row = norm_gain.reshape(1, width)
    ids = expert_ids.reshape(tokens, 2).T
    gates = gate_weights.reshape(tokens, 2).T
    send = on_chip(
        functools.partial(dispatch_kernel, experts),
        sds((experts * 2 * CAP, width)),
        [x_rows, gain_row, cot_rows, ids, gates],
        us=2.5,
        after=[give_w],
    )
    arrived = lax.all_to_all(
        send.reshape(experts, 2 * CAP, width), ("seq", "dp"), 0, 0, tiled=True
    )
    own_w = pick(at, w_t, [send], 1)

    from_prev = shift(arrived, "expert", 1)
    from_next = shift(arrived, "expert", -1)
    cut = experts // 2
    sel = (sel_x, sel_s)
    n_q, n_m = positions, mem_rows
    own_half = expert_piece([arrived], [own_w], sel, [])
    relays = on_chip(
        cut_kernel,
        [sds((cut, 2 * CAP, width))] * 2,
        [from_prev, from_next],
        us=0.5,
        after=[own_half[0], got_w],
    )
    far = [shift(relays[0], "expert", 1), shift(relays[1], "expert", -1)]
    qkv = on_chip(
        pack_kernel,
        sds((2 * width // 128, 2 * (n_q + 2 * n_m), 128)),
        [a.reshape(-1, width) for a in (queries, memory_keys, memory_values)],
        us=0.5,
        after=[relays[0]],
    )
    after = [qkv]
    qkv = lax.all_to_all(qkv, "seq", 0, 0, tiled=True)
    results = []
    for part in (from_prev, from_next):
        results.append(expert_piece([part], [own_w, got_w], sel, after))
        after = [results[-1][0]]
    results.append(expert_piece(far, [own_w, got_w], sel, after))
    back, saved2 = second_half(own_half[1], got_w, own_half[0], [results[-1][0]])
    results.append((back, *own_half[1:], saved2))
    backs = [
        shift(res[0], "expert", -by) if by else res[0]
        for by, res in zip((1, -1, 2, 0), results)
    ]
    theirs = weight_grads(results, 1, [])
    got_grads = [xor_swap(theirs[0], "dp", 1)]
    mine = weight_grads(results, 0, [theirs[0]])
    payload = on_chip(
        payload_kernel,
        sds((experts * BACK, width)),
        [spread, lines, lanes, results[3][1], *backs],
        us=2,
        after=[mine[0], got_grads[0]],
    )
    payload, send_grads = lax.optimization_barrier((payload, theirs[1]))
    got_grads.append(xor_swap(send_grads, "dp", 1))
    returned = lax.all_to_all(
        payload.reshape(experts, BACK, width), ("seq", "dp"), 0, 0, tiled=True
    )
    probs0, o0 = attn_forward(qkv, 0, n_q, n_m, logit_scale, [payload])
    probs1, o1 = attn_forward(qkv, 1, n_q, n_m, logit_scale, [o0])

    stream_grad, heads_grad, gain_grad, gates_grad = on_chip(
        functools.partial(combine_kernel, experts),
        [
            sds((tokens, width)),
            sds((2 * width // 128, tokens // 2, 128)),
            sds((1, width), F32),
            sds((tokens, 2), F32),
        ],
        [returned.reshape(experts * BACK, width), x_rows, gain_row, cot_rows, ids, gates],
        us=2,
        after=[o1, got_grads[1]],
    )
    heads_grad = lax.all_to_all(heads_grad, "seq", 0, 0, tiled=True)
    heads_grad, send_grads = lax.optimization_barrier((heads_grad, theirs[2]))
    got_grads.append(xor_swap(send_grads, "dp", 1))
    for bits in (1, 2):
        gain_grad = gain_grad + xor_swap(gain_grad, "expert", bits)

    out = attn_backward(
        qkv, heads_grad, (probs0, probs1), (o0, o1), n_q, n_m, logit_scale, []
    )
    out, got_grads[2] = lax.optimization_barrier((out, got_grads[2]))
    w_grads = place(at, mine, got_grads, [])
    w_grads = [jnp.swapaxes(w_grads[0], 1, 2), jnp.swapaxes(w_grads[1], 1, 2), w_grads[2]]
    out = lax.all_to_all(out, "seq", 0, 0, tiled=True)
    shapes = [(examples * n, width) for n in (n_q, n_m, n_m)]
    d_q, d_k, d_v = on_chip(unpack_kernel, [sds(s) for s in shapes], [out], us=2)
    return (
        d_q.reshape(queries.shape),
        d_k.reshape(memory_keys.shape),
        d_v.reshape(memory_values.shape),
        stream_grad.reshape(stream.shape),
        gain_grad.reshape(width),
        *w_grads,
        gates_grad.reshape(gate_weights.shape),
    )


def solution(mesh):
    rows = P(("expert", "dp"), "seq", None)
    wide = P("seq", None, ("expert", "dp"))
    deep = P("seq", ("expert", "dp"), None)
    pairs = P("seq", ("expert", "dp"), None, None)
    in_specs = (rows, rows, rows, rows, P(), wide, wide, deep, pairs, pairs, rows)
    out_specs = (rows, rows, rows, rows, P(), wide, wide, deep, pairs)
    return jax.shard_map(
        on_device, mesh=mesh, in_specs=in_specs, out_specs=out_specs, check_vma=False
    )
```

```python
import functools

import jax
import jax.numpy as jnp
import numpy as np
from jax import lax
from jax.experimental import pallas as pl
from jax.experimental.pallas import tpu as pltpu
from jax.sharding import PartitionSpec as P

HEADS = 16
EPSILON = 1e-06
CAP = 12
BACK = 16
GROUP = 8
F32 = jnp.float32
BF16 = jnp.bfloat16
HBM = pl.BlockSpec(memory_space=pltpu.HBM)


def lasts(us):
    return pl.CostEstimate(flops=1, bytes_accessed=int(us * 3.2e6), transcendentals=0)


def dot(a, b, ca=1, cb=0):
    return lax.dot_general(a, b, (((ca,), (cb,)), ((), ())), preferred_element_type=F32)


def xor_swap(value, axis, bits):
    size = lax.axis_size(axis)
    return lax.ppermute(value, axis, [(i, i ^ bits) for i in range(size)])


def shift(value, axis, by):
    size = lax.axis_size(axis)
    return lax.ppermute(value, axis, [(i, (i + by) % size) for i in range(size)])


def on_chip(kernel, out_shape, args, *, us, after=(), vmem=16, scratch=(), far_in=(), far_out=()):
    count = len(args)
    near = pl.BlockSpec(memory_space=pltpu.VMEM)
    outs = out_shape if isinstance(out_shape, list) else [out_shape]
    outs = [pltpu.HBM(o.shape, o.dtype) if i in far_out else o for i, o in enumerate(outs)]
    args = [stay(a) if i in far_in else a for i, a in enumerate(args)]

    def body(*refs):
        kernel(*refs[:count], *refs[count + len(after) :])

    result = pl.pallas_call(
        body,
        out_shape=outs,
        in_specs=[HBM if i in far_in else near for i in range(count)]
        + [pl.BlockSpec(memory_space=pl.ANY)] * len(after),
        out_specs=[HBM if i in far_out else near for i in range(len(outs))],
        scratch_shapes=list(scratch),
        compiler_params=pltpu.CompilerParams(vmem_limit_bytes=vmem << 20),
        cost_estimate=lasts(us),
    )(*args, *after)
    return list(result) if isinstance(out_shape, list) else result[0]


def stay(array):
    return pltpu.with_memory_space_constraint(array, pltpu.HBM)


def sds(shape, dtype=BF16):
    return jax.ShapeDtypeStruct(shape, dtype)


def iota(shape, dim):
    return lax.broadcasted_iota(jnp.int32, shape, dim)


def mask(cond):
    return jnp.where(cond, 1.0, 0.0).astype(BF16)


def dispatch_kernel(experts, x_ref, gain_ref, cot_ref, idt_ref, gt_ref, send_ref):
    tokens = x_ref.shape[0]
    x = x_ref[...].astype(F32)
    inverse = lax.rsqrt(jnp.mean(x * x, axis=-1, keepdims=True) + EPSILON)
    normed = (x * inverse * gain_ref[...]).astype(BF16)
    e_of = iota((experts, tokens), 0)
    hot = [idt_ref[k : k + 1, :] == e_of for k in range(2)]
    before = mask(iota((tokens, tokens), 0) < iota((tokens, tokens), 1))
    count = dot(mask(hot[0] | hot[1]), before)
    rows = experts * 2 * CAP
    r_of = iota((rows, tokens), 0)
    plain, weighted = None, 0.0
    for k in range(2):
        slot = jnp.sum(jnp.where(hot[k], count, 0.0), axis=0, keepdims=True)
        at = idt_ref[k : k + 1, :] * (2 * CAP) + slot.astype(jnp.int32)
        here = r_of == at
        plain = here if plain is None else plain | here
        g = gt_ref[k : k + 1, :].astype(F32)
        weighted = weighted + jnp.where(r_of == at + CAP, g, 0.0)
    choose = jnp.concatenate([mask(plain), weighted.astype(BF16)], axis=1)
    sources = jnp.concatenate([normed, cot_ref[...]], axis=0)
    send_ref[...] = dot(choose, sources).astype(BF16)


def pick(at, weights, after, us):
    _, hid, width = weights[0].shape
    count = len(weights)

    def body(at_ref, *refs):
        out_ref, sems = refs[-2:]
        copies = [
            pltpu.make_async_copy(ref.at[at_ref[0]], out_ref.at[kind], sems.at[kind])
            for kind, ref in enumerate(refs[:count])
        ]
        for copy in copies:
            copy.start()
        for copy in copies:
            copy.wait()

    return pl.pallas_call(
        body,
        in_specs=[pl.BlockSpec(memory_space=pltpu.SMEM)]
        + [HBM] * count
        + [pl.BlockSpec(memory_space=pl.ANY)] * len(after),
        out_specs=pl.BlockSpec(memory_space=pltpu.VMEM),
        out_shape=sds((count, hid, width)),
        scratch_shapes=[pltpu.SemaphoreType.DMA((count,))],
        compiler_params=pltpu.CompilerParams(vmem_limit_bytes=16 << 20),
        cost_estimate=lasts(us),
    )(at, *[stay(w) for w in weights], *after)


def place(at, mine, got, after):
    kinds = len(mine)
    hid, width = mine[0].shape
    moves, kind, row = [], 0, 0
    for part, array in enumerate(got):
        first = 0
        while first < array.shape[0]:
            size = min(hid - row, array.shape[0] - first)
            moves.append((kind, row, part, first, size))
            first, row = first + size, row + size
            if row == hid:
                kind, row = kind + 1, 0
    count = kinds + len(got)

    def body(at_ref, *refs):
        mine_refs, got_refs = refs[:kinds], refs[kinds:count]
        outs, sems = refs[count + len(after) : -1], refs[-1]
        at = at_ref[0]
        copies = []
        for k, out in enumerate(outs):
            copies.append(pltpu.make_async_copy(mine_refs[k], out.at[at], sems.at[k]))
        for i, (k, to, part, first, rows) in enumerate(moves):
            copies.append(
                pltpu.make_async_copy(
                    got_refs[part].at[pl.ds(first, rows), :],
                    outs[k].at[1 - at, pl.ds(to, rows), :],
                    sems.at[kinds + i],
                )
            )
        for copy in copies:
            copy.start()
        for copy in copies:
            copy.wait()

    return pl.pallas_call(
        body,
        out_shape=[pltpu.HBM((2, hid, width), BF16)] * kinds,
        in_specs=[pl.BlockSpec(memory_space=pltpu.SMEM)]
        + [pl.BlockSpec(memory_space=pltpu.VMEM)] * count
        + [pl.BlockSpec(memory_space=pl.ANY)] * len(after),
        out_specs=[HBM] * kinds,
        scratch_shapes=[pltpu.SemaphoreType.DMA((kinds + len(moves),))],
        compiler_params=pltpu.CompilerParams(vmem_limit_bytes=4 << 20),
        cost_estimate=lasts(3),
    )(at, *mine, *got, *after)


def separate(sx_ref, ss_ref, part_ref, xs_ref, j):
    step = GROUP * CAP
    for i in range(part_ref.shape[0] // (2 * step)):
        block = part_ref[2 * step * i : 2 * step * (i + 1), :]
        at = slice(step * j, step * (j + 1))
        xs_ref[0, at, :] = dot(sx_ref[...], block).astype(BF16)
        xs_ref[1, at, :] = dot(ss_ref[...], block).astype(BF16)
        j += 1
    return j


def hidden_block(xs_ref, w_ref, saved_ref):
    pre_gate = dot(xs_ref[0], w_ref[0], 1, 1)
    pre_up = dot(xs_ref[0], w_ref[1], 1, 1)
    d_hidden = dot(xs_ref[1], w_ref[2], 1, 1)
    cdf = 0.5 * (1.0 + lax.erf(pre_gate * 0.7071067811865476))
    pdf = jnp.exp(-0.5 * pre_gate * pre_gate) * 0.3989422804014327
    activated = pre_gate * cdf
    hidden = (activated * pre_up).astype(BF16)
    d_gate = (d_hidden * pre_up * (cdf + pre_gate * pdf)).astype(BF16)
    d_up = (d_hidden * activated).astype(BF16)
    for kind, value in enumerate((d_gate, d_up, hidden)):
        saved_ref[kind] = value
    rows = dot(d_gate, w_ref[0]) + dot(d_up, w_ref[1])
    return rows, jnp.sum(hidden.astype(F32) * d_hidden, axis=1, keepdims=True)


def put_back(back_ref, total, gate):
    rows = total.shape[0]
    back_ref[:rows, :] = total.astype(BF16)
    spread = jnp.broadcast_to(gate, (rows, 128)).T
    back_ref[rows:, :rows] = spread[:16, :].astype(BF16)
    back_ref[rows:, rows:] = jnp.zeros((16, back_ref.shape[1] - rows), BF16)


def piece_kernel(count, sx_ref, ss_ref, *refs):
    parts, refs = refs[:count], refs[count:]
    blocks = (len(refs) - 6) // 2
    weights, refs = refs[:blocks], refs[blocks:]
    back_ref, xs_out, refs = refs[0], refs[1], refs[2:]
    saved_outs, (part_scr, xs_ref, saved_ref), sems = refs[:blocks], refs[blocks:-1], refs[-1]
    size = parts[0].shape[0]
    fetches = [
        pltpu.make_async_copy(p, part_scr.at[pl.ds(size * i, size), :], sems.at[i])
        for i, p in enumerate(parts)
    ]
    for fetch in fetches:
        fetch.start()
    j = 0
    for i, fetch in enumerate(fetches):
        fetch.wait()
        j = separate(sx_ref, ss_ref, part_scr.at[pl.ds(size * i, size), :], xs_ref, j)
    stores = [pltpu.make_async_copy(xs_ref, xs_out, sems.at[count])]
    stores[0].start()
    total, gate = None, None
    for n, w_ref in enumerate(weights):
        rows, terms = hidden_block(xs_ref, w_ref, saved_ref.at[n])
        stores.append(
            pltpu.make_async_copy(saved_ref.at[n], saved_outs[n], sems.at[count + 1 + n])
        )
        stores[-1].start()
        total = rows if n == 0 else total + rows
        gate = terms if n == 0 else gate + terms
    put_back(back_ref, total, gate)
    for store in stores:
        store.wait()


def second_half_kernel(xs_in, w_ref, part_ref, back_ref, saved_out, xs_ref, saved_ref, sems):
    fetch = pltpu.make_async_copy(xs_in, xs_ref, sems.at[0])
    fetch.start()
    fetch.wait()
    total, gate = hidden_block(xs_ref, w_ref, saved_ref)
    store = pltpu.make_async_copy(saved_ref, saved_out, sems.at[1])
    store.start()
    put_back(back_ref, total, gate)
    back_ref[...] = (back_ref[...].astype(F32) + part_ref[...].astype(F32)).astype(BF16)
    store.wait()


def expert_piece(parts, weights, sel, after):
    width = parts[0].shape[-1]
    parts = [p.reshape(-1, width) for p in parts]
    rows = sum(p.shape[0] for p in parts) // 2
    hid = weights[0].shape[1]
    blocks, count = len(weights), len(parts)
    return on_chip(
        functools.partial(piece_kernel, count),
        [sds((rows + 16, width)), sds((2, rows, width))] + [sds((3, rows, hid))] * blocks,
        [*sel, *parts, *weights],
        us=0.5,
        vmem=24,
        after=after,
        scratch=[
            pltpu.VMEM((2 * rows, width), BF16),
            pltpu.VMEM((2, rows, width), BF16),
            pltpu.VMEM((blocks, 3, rows, hid), BF16),
            pltpu.SemaphoreType.DMA((count + 1 + blocks,)),
        ],
        far_in=range(2, 2 + count),
        far_out=range(1, 2 + blocks),
    )


def second_half(xs, got_w, part, after):
    saved = (3, xs.shape[1], got_w.shape[1])
    return on_chip(
        second_half_kernel,
        [sds(part.shape), sds(saved)],
        [xs, got_w, part],
        us=0.5,
        after=after,
        scratch=[
            pltpu.VMEM(xs.shape, BF16),
            pltpu.VMEM(saved, BF16),
            pltpu.SemaphoreType.DMA((2,)),
        ],
        far_in=(0,),
        far_out=(1,),
    )


def weight_kernel(n, hid, kinds, *refs):
    count = len(kinds)
    ins, outs = refs[: 2 * n], refs[2 * n : -3]
    xs_ref, saved_ref, sems = refs[-3:]
    low, high = kinds[0] // 2, kinds[-1] // 2
    rows = saved_ref.shape[1] // n
    fetches = []
    for z in range(n):
        at = pl.ds(rows * z, rows)
        moves = (
            (ins[2 * z].at[pl.ds(low, high + 1 - low)], xs_ref),
            (ins[2 * z + 1].at[pl.ds(kinds[0], count)], saved_ref),
        )
        for i, (src, ref) in enumerate(moves):
            fetches.append(pltpu.make_async_copy(src, ref.at[:, at, :], sems.at[2 * z + i]))
            fetches[-1].start()
    for fetch in fetches:
        fetch.wait()
    part, to = 0, 0
    for i, kind in enumerate(kinds):
        total = dot(saved_ref[i], xs_ref[kind // 2 - low], 0, 0).astype(BF16)
        at = 0
        while at < hid:
            size = min(hid - at, outs[part].shape[0] - to)
            outs[part][to : to + size, :] = total[at : at + size, :]
            at, to = at + size, to + size
            if to == outs[part].shape[0]:
                part, to = part + 1, 0


def weight_grads(results, half, hid, kinds, parts, after):
    xs, saved = results[0][1:3]
    n, (_, rows, padded), width = len(results), saved.shape, xs.shape[2]
    count = len(kinds)
    inputs = kinds[-1] // 2 + 1 - kinds[0] // 2
    return on_chip(
        functools.partial(weight_kernel, n, hid, kinds),
        [sds((part, width)) for part in parts],
        [a for r in results for a in (r[1], r[2 + half])],
        us=0.5,
        vmem=16,
        after=after,
        scratch=[
            pltpu.VMEM((inputs, n * rows, width), BF16),
            pltpu.VMEM((count, n * rows, padded), BF16),
            pltpu.SemaphoreType.DMA((2 * n,)),
        ],
        far_in=range(2 * n),
    )


def payload_kernel(spread_ref, ga_ref, gb_ref, xs_ref, a_ref, b_ref, c_ref, d_ref, out_ref):
    rows = a_ref.shape[0] - 16
    step = GROUP * CAP
    total = (a_ref[...].astype(F32) + b_ref[...].astype(F32)) + (
        c_ref[...].astype(F32) + d_ref[...].astype(F32)
    )
    gates = total[rows : rows + 1, :rows]
    total = total[:rows, :]
    gain = jnp.sum(total * xs_ref[0].astype(F32), axis=0, keepdims=True)
    coarse = gain.astype(BF16)
    fine = (gain - coarse.astype(F32)).astype(BF16)
    order = iota((16, gain.shape[1]), 0)
    gains = jnp.where(order == 0, coarse.astype(F32), 0.0) + jnp.where(
        order == 1, fine.astype(F32), 0.0
    )
    gains = gains.astype(BF16)
    total = total.astype(BF16)
    wide = GROUP * BACK
    for j in range(rows // step):
        block = jnp.concatenate([total[step * j : step * (j + 1), :], gains], axis=0)
        out_ref[wide * j : wide * (j + 1), :] = dot(spread_ref[...], block).astype(BF16)
    placed = dot((ga_ref[...].astype(F32) * gates).astype(BF16), gb_ref[...]).astype(BF16)
    out_ref[:, :128] = out_ref[:, :128] + placed


def column(row):
    count = row.shape[1]
    return jnp.broadcast_to(row, (count, count)).T[:, :1]


def combine_kernel(
    experts, r_ref, x_ref, gain_ref, cot_ref, idt_ref, gt_ref, out_ref, heads_ref, gain_out, gates_out
):
    tokens = x_ref.shape[0]
    e_of = iota((tokens, experts), 1)
    ids = [column(idt_ref[k : k + 1, :].astype(F32)).astype(jnp.int32) for k in range(2)]
    hot = [i == e_of for i in ids]
    before = mask(iota((tokens, tokens), 1) < iota((tokens, tokens), 0))
    count = dot(before, mask(hot[0] | hot[1]))
    slots = [
        jnp.sum(jnp.where(h, count, 0.0), axis=1, keepdims=True).astype(jnp.int32) for h in hot
    ]
    r_of = iota((tokens, experts * BACK), 1)
    take = mask((r_of == ids[0] * BACK + slots[0]) | (r_of == ids[1] * BACK + slots[1]))
    d_normed = dot(take, r_ref[...])
    lane = iota((tokens, 128), 1)
    for k in range(2):
        line = dot(mask(r_of == ids[k] * BACK + CAP), r_ref[:, :128])
        found = jnp.sum(jnp.where(lane == slots[k], line, 0.0), axis=1, keepdims=True)
        gates_out[:, k : k + 1] = found / column(gt_ref[k : k + 1, :].astype(F32))
    gain = gain_ref[...]
    line_of = iota((16, experts * BACK), 1) % BACK
    sums = dot(mask((line_of == CAP + 1) | (line_of == CAP + 2)), r_ref[...])
    gain_out[...] = sums[:1, :] / gain
    x = x_ref[...].astype(F32)
    inverse = lax.rsqrt(jnp.mean(x * x, axis=-1, keepdims=True) + EPSILON)
    unit = x * inverse
    scaled = d_normed * gain
    grad = cot_ref[...].astype(F32) + inverse * (
        scaled - unit * jnp.mean(scaled * unit, axis=-1, keepdims=True)
    )
    grad = grad.astype(BF16)
    out_ref[...] = grad
    put_heads(heads_ref, 0, grad)


def put_heads(out_ref, offset, rows):
    half = rows.shape[0] // 2
    count = rows.shape[1] // 128
    for pair in range(2):
        for head in range(count):
            out_ref[pair * count + head, offset : offset + half, :] = rows[
                pair * half : (pair + 1) * half, head * 128 : (head + 1) * 128
            ]


def pack_kernel(*refs):
    srcs, out_ref, held, sems = refs[:3], refs[3], refs[4:7], refs[7]
    fetches = [
        pltpu.make_async_copy(src, ref, sems.at[i]) for i, (src, ref) in enumerate(zip(srcs, held))
    ]
    for fetch in fetches:
        fetch.start()
    offset = 0
    for fetch, ref in zip(fetches, held):
        fetch.wait()
        put_heads(out_ref, offset, ref)
        offset += ref.shape[0] // 2


def pack(arrays, after):
    rows = sum(a.shape[0] for a in arrays) // 2
    width = arrays[0].shape[1]
    return on_chip(
        pack_kernel,
        sds((2 * width // 128, rows, 128)),
        arrays,
        us=0.5,
        after=after,
        scratch=[pltpu.VMEM(a.shape, BF16) for a in arrays] + [pltpu.SemaphoreType.DMA((3,))],
        far_in=range(3),
    )


def unpack_kernel(in_ref, *outs):
    offset = 0
    for ref in outs:
        half = ref.shape[0] // 2
        count = ref.shape[1] // 128
        for pair in range(2):
            for head in range(count):
                ref[pair * half : (pair + 1) * half, head * 128 : (head + 1) * 128] = in_ref[
                    pair * count + head, offset : offset + half, :
                ]
        offset += half


def cut_kernel(prev_ref, next_ref, low_ref, high_ref):
    half = low_ref.shape[0]
    low_ref[...] = prev_ref[:half]
    high_ref[...] = next_ref[half:]


def attn_forward_kernel(n_q, n_m, scale, b, qkv_ref, p_out, o_ref, s_scr, p_ref, sems):
    seq = qkv_ref.shape[0]
    lq = seq * n_q
    per = 2
    chunk = per * n_m
    count = seq // per
    q = qkv_ref[:, pl.ds(b * n_q, n_q), :].reshape(lq, 128)
    qt = (q.astype(F32) * scale).T
    half_of = iota((128, lq), 0) < 64
    k_at = 2 * n_q + b * n_m
    v_at = 2 * n_q + 2 * n_m + b * n_m
    for h in range(2):
        qh = jnp.where(half_of if h == 0 else jnp.logical_not(half_of), qt, 0.0).astype(BF16)

        def score(c, peak):
            k = qkv_ref[pl.ds(c * per, per), pl.ds(k_at, n_m), :].reshape(chunk, 128)
            s = dot(k, qh)
            s_scr[pl.ds(pl.multiple_of(c * chunk, chunk), chunk), :] = s
            return jnp.maximum(peak, jnp.max(s, axis=0, keepdims=True))

        peak = lax.fori_loop(0, count, score, jnp.full((1, lq), -jnp.inf, F32))

        def power(c, total):
            at = pl.ds(pl.multiple_of(c * chunk, chunk), chunk)
            e = jnp.exp(s_scr[at, :] - peak)
            s_scr[at, :] = e
            return total + jnp.sum(e, axis=0, keepdims=True)

        total = lax.fori_loop(0, count, power, jnp.zeros((1, lq), F32))
        factor = 1.0 / total

        def finish(c, out):
            at = pl.ds(pl.multiple_of(c * chunk, chunk), chunk)
            p = (s_scr[at, :] * factor).astype(BF16)
            p_ref[h, at, :] = p
            v = qkv_ref[pl.ds(c * per, per), pl.ds(v_at, n_m), :].reshape(chunk, 128)
            vt = v.astype(F32).T.astype(BF16)
            return out + dot(vt[64 * h : 64 * h + 64, :], p)

        o_ref[64 * h : 64 * h + 64, :] = lax.fori_loop(
            0, count, finish, jnp.zeros((64, lq), F32)
        )
        pltpu.make_async_copy(p_ref.at[h], p_out.at[h], sems.at[h]).start()
    for h in range(2):
        pltpu.make_async_copy(p_ref.at[h], p_out.at[h], sems.at[h]).wait()


def attn_backward_kernel(
    n_q, n_m, scale, qkv_ref, do_ref, p0_ref, p1_ref, o0_ref, o1_ref, out_ref, dq_scr, p_scr, sems
):
    seq = qkv_ref.shape[0]
    lq = seq * n_q
    per = 4
    chunk = per * n_m
    lane = iota((lq, 128), 1) < 64
    row = iota((128, lq), 0) < 64
    zero = jnp.zeros((), BF16)
    p_refs = (p0_ref, p1_ref)

    def fetch(b, c):
        at = pl.ds(c * chunk, chunk)
        return pltpu.make_async_copy(p_refs[b].at[:, at, :], p_scr.at[b, :, at, :], sems.at[b, c])

    for b in range(2):
        for c in range(seq // per):
            fetch(b, c).start()
    for b, o_ref in enumerate((o0_ref, o1_ref)):
        q_at = pl.ds(b * n_q, n_q)
        k_at = pl.ds(2 * n_q + b * n_m, n_m)
        v_at = pl.ds(2 * n_q + 2 * n_m + b * n_m, n_m)
        d_out = do_ref[:, q_at, :].reshape(lq, 128)
        dt = d_out.astype(F32).T
        prod = dt * o_ref[...]
        delta = [jnp.sum(prod[64 * h : 64 * h + 64, :], axis=0, keepdims=True) for h in range(2)]
        dt = dt.astype(BF16)
        q = (qkv_ref[:, q_at, :].reshape(lq, 128).astype(F32) * scale).astype(BF16)
        rows_of = [jnp.where(row, dt, zero), jnp.where(row, zero, dt)]
        d_out_of = [jnp.where(lane, d_out, zero), jnp.where(lane, zero, d_out)]
        q_of = [jnp.where(lane, q, zero), jnp.where(lane, zero, q)]
        dq_scr[...] = jnp.zeros_like(dq_scr)

        for c in range(seq // per):
            src = pl.ds(c * per, per)
            at = pl.ds(c * chunk, chunk)
            fetch(b, c).wait()
            k = qkv_ref[src, k_at, :].reshape(chunk, 128)
            v = qkv_ref[src, v_at, :].reshape(chunk, 128)
            kt = k.astype(F32).T.astype(BF16)
            dk, dv = None, None
            for h in range(2):
                d_p = dot(v, rows_of[h])
                p = p_scr[b, h, at, :]
                ds = (p.astype(F32) * (d_p - delta[h])).astype(BF16)
                dv_h = dot(p, d_out_of[h])
                dk_h = dot(ds, q_of[h])
                dv = dv_h if dv is None else dv + dv_h
                dk = dk_h if dk is None else dk + dk_h
                mine = slice(64 * h, 64 * h + 64)
                dq_scr[mine, :] += dot(kt[mine, :], ds)
            out_ref[src, k_at, :] = dk.astype(BF16).reshape(per, n_m, 128)
            out_ref[src, v_at, :] = dv.astype(BF16).reshape(per, n_m, 128)
        dq = (dq_scr[...] * scale).T.astype(BF16)
        out_ref[:, q_at, :] = dq.reshape(seq, n_q, 128)


def attn_forward(qkv, example, n_q, n_m, scale, after):
    seq = qkv.shape[0]
    lq, lm = seq * n_q, seq * n_m
    return on_chip(
        functools.partial(attn_forward_kernel, n_q, n_m, scale, example),
        [sds((2, lm, lq)), sds((128, lq), F32)],
        [qkv],
        us=8.7,
        after=after,
        scratch=[
            pltpu.VMEM((lm, lq), F32),
            pltpu.VMEM((2, lm, lq), BF16),
            pltpu.SemaphoreType.DMA((2,)),
        ],
        far_out=(0,),
    )


def attn_backward(qkv, d_out, probs, o_t, n_q, n_m, scale, after):
    seq = qkv.shape[0]
    lq = seq * n_q
    return on_chip(
        functools.partial(attn_backward_kernel, n_q, n_m, scale),
        sds(qkv.shape),
        [qkv, d_out, *probs, *o_t],
        us=11,
        after=after,
        vmem=24,
        scratch=[
            pltpu.VMEM((128, lq), F32),
            pltpu.VMEM((2, 2, seq * n_m, lq), BF16),
            pltpu.SemaphoreType.DMA((2, seq // 4)),
        ],
        far_in=(2, 3),
    )


def selections(experts):
    r = np.arange(GROUP * CAP)
    c = np.arange(2 * GROUP * CAP)
    first = c[None, :] == ((r // CAP) * 2 * CAP + r % CAP)[:, None]
    second = c[None, :] == ((r // CAP) * 2 * CAP + r % CAP + CAP)[:, None]
    o = np.arange(GROUP * BACK)
    spread = (r[None, :] == ((o // BACK) * CAP + o % BACK)[:, None]) & (o % BACK < CAP)[:, None]
    extra = (o % BACK)[:, None] == (CAP + 1 + np.arange(16))[None, :]
    spread = np.concatenate([spread, extra], axis=1)
    o_all = np.arange(experts * BACK)
    c_all = np.arange(experts * CAP)
    lines = (o_all % BACK == CAP)[:, None] & (c_all[None, :] // CAP == o_all[:, None] // BACK)
    lanes = c_all[:, None] % CAP == np.arange(128)[None, :]
    return [jnp.asarray(m.astype(np.float32), BF16) for m in (first, second, spread, lines, lanes)]


def on_device(
    queries,
    memory_keys,
    memory_values,
    stream,
    norm_gain,
    gate_proj,
    up_proj,
    down_proj,
    expert_ids,
    gate_weights,
    upstream_grad,
):
    examples, positions, width = stream.shape
    mem_rows = memory_keys.shape[1]
    tokens = examples * positions
    experts = lax.axis_size("seq") * gate_proj.shape[0]
    logit_scale = (width // HEADS) ** (-0.5)
    my_dp = lax.axis_index("dp")
    sel_x, sel_s, spread, lines, lanes = selections(experts)

    w_t = [jnp.swapaxes(gate_proj, 1, 2), jnp.swapaxes(up_proj, 1, 2), down_proj]
    hid = w_t[2].shape[1]
    at = my_dp.reshape(1).astype(jnp.int32)
    give_w = pick(1 - at, w_t, [], 1)
    got_w = xor_swap(give_w, "dp", 1)

    x_rows = stream.reshape(tokens, width)
    cot_rows = upstream_grad.reshape(tokens, width)
    gain_row = norm_gain.reshape(1, width)
    ids = expert_ids.reshape(tokens, 2).T
    gates = gate_weights.reshape(tokens, 2).T
    send = on_chip(
        functools.partial(dispatch_kernel, experts),
        sds((experts * 2 * CAP, width)),
        [x_rows, gain_row, cot_rows, ids, gates],
        us=2.5,
        after=[give_w],
    )
    arrived = lax.all_to_all(
        send.reshape(experts, 2 * CAP, width), ("seq", "dp"), 0, 0, tiled=True
    )
    own_w = pick(at, w_t, [send], 1)

    from_prev = shift(arrived, "expert", 1)
    from_next = shift(arrived, "expert", -1)
    cut = experts // 2
    sel = (sel_x, sel_s)
    n_q, n_m = positions, mem_rows
    own_half = expert_piece([arrived], [own_w], sel, [])
    packed = pack(
        [a.reshape(-1, width) for a in (queries, memory_keys, memory_values)], [own_half[0]]
    )
    relays = on_chip(
        cut_kernel,
        [sds((cut, 2 * CAP, width))] * 2,
        [from_prev, from_next],
        us=0.5,
        after=[packed, got_w],
    )
    far = [shift(relays[0], "expert", 1), shift(relays[1], "expert", -1)]
    packed, first_cut = lax.optimization_barrier((packed, relays[0]))
    after = [first_cut]
    qkv = lax.all_to_all(packed, "seq", 0, 0, tiled=True)
    results = []
    for part in (from_prev, from_next):
        results.append(expert_piece([part], [own_w, got_w], sel, after))
        after = [results[-1][0]]
    back, saved2 = second_half(own_half[1], got_w, own_half[0], after)
    results.append((back, *own_half[1:], saved2))
    results.append(expert_piece(far, [own_w, got_w], sel, [back]))
    backs = [
        shift(res[0], "expert", -by) if by else res[0]
        for by, res in zip((1, -1, 0, 2), results)
    ]
    theirs = weight_grads(results, 1, hid, (0,), (hid,), [])
    got_grads = [xor_swap(theirs[0], "dp", 1)]
    theirs += weight_grads(results, 1, hid, (1, 2), (hid, hid // 2, hid // 2), theirs)
    payload = on_chip(
        payload_kernel,
        sds((experts * BACK, width)),
        [spread, lines, lanes, results[2][1], *backs],
        us=2,
        after=[theirs[1], got_grads[0]],
    )
    payload, send_grads = lax.optimization_barrier((payload, theirs[1]))
    got_grads.append(xor_swap(send_grads, "dp", 1))
    returned = lax.all_to_all(
        payload.reshape(experts, BACK, width), ("seq", "dp"), 0, 0, tiled=True
    )
    probs0, o0 = attn_forward(qkv, 0, n_q, n_m, logit_scale, [payload])
    probs1, o1 = attn_forward(qkv, 1, n_q, n_m, logit_scale, [o0])

    stream_grad, heads_grad, gain_grad, gates_grad = on_chip(
        functools.partial(combine_kernel, experts),
        [
            sds((tokens, width)),
            sds((2 * width // 128, tokens // 2, 128)),
            sds((1, width), F32),
            sds((tokens, 2), F32),
        ],
        [returned.reshape(experts * BACK, width), x_rows, gain_row, cot_rows, ids, gates],
        us=2,
        after=[o1, got_grads[1]],
    )
    heads_grad = lax.all_to_all(heads_grad, "seq", 0, 0, tiled=True)
    heads_grad, *send_grads = lax.optimization_barrier((heads_grad, theirs[2], theirs[3]))
    got_grads += [xor_swap(part, "dp", 1) for part in send_grads]
    for bits in (1, 2):
        gain_grad = gain_grad + xor_swap(gain_grad, "expert", bits)

    out = attn_backward(
        qkv, heads_grad, (probs0, probs1), (o0, o1), n_q, n_m, logit_scale, []
    )
    out, got_grads[2], got_grads[3] = lax.optimization_barrier((out, got_grads[2], got_grads[3]))
    mine = weight_grads(results, 0, hid, (0, 1, 2), (hid,) * 3, [out])
    w_grads = place(at, mine, got_grads, [])
    w_grads = [jnp.swapaxes(w_grads[0], 1, 2), jnp.swapaxes(w_grads[1], 1, 2), w_grads[2]]
    out = lax.all_to_all(out, "seq", 0, 0, tiled=True)
    shapes = [(examples * n, width) for n in (n_q, n_m, n_m)]
    d_q, d_k, d_v = on_chip(unpack_kernel, [sds(s) for s in shapes], [out], us=2)
    return (
        d_q.reshape(queries.shape),
        d_k.reshape(memory_keys.shape),
        d_v.reshape(memory_values.shape),
        stream_grad.reshape(stream.shape),
        gain_grad.reshape(width),
        *w_grads,
        gates_grad.reshape(gate_weights.shape),
    )


def solution(mesh):
    rows = P(("expert", "dp"), "seq", None)
    wide = P("seq", None, ("expert", "dp"))
    deep = P("seq", ("expert", "dp"), None)
    pairs = P("seq", ("expert", "dp"), None, None)
    in_specs = (rows, rows, rows, rows, P(), wide, wide, deep, pairs, pairs, rows)
    out_specs = (rows, rows, rows, rows, P(), wide, wide, deep, pairs)
    return jax.shard_map(
        on_device, mesh=mesh, in_specs=in_specs, out_specs=out_specs, check_vma=False
    )
```

```python
import functools

import jax
import jax.numpy as jnp
import numpy as np
from jax import lax
from jax.experimental import pallas as pl
from jax.experimental.pallas import tpu as pltpu
from jax.sharding import PartitionSpec as P

HEADS = 16
EPSILON = 1e-06
CAP = 12
BACK = 16
GROUP = 8
F32 = jnp.float32
BF16 = jnp.bfloat16
HBM = pl.BlockSpec(memory_space=pltpu.HBM)


def lasts(us):
    return pl.CostEstimate(flops=1, bytes_accessed=int(us * 3.2e6), transcendentals=0)


def dot(a, b, ca=1, cb=0):
    return lax.dot_general(a, b, (((ca,), (cb,)), ((), ())), preferred_element_type=F32)


def xor_swap(value, axis, bits):
    size = lax.axis_size(axis)
    return lax.ppermute(value, axis, [(i, i ^ bits) for i in range(size)])


def shift(value, axis, by):
    size = lax.axis_size(axis)
    return lax.ppermute(value, axis, [(i, (i + by) % size) for i in range(size)])


def on_chip(
    kernel, out_shape, args, *, us, after=(), behind=(), vmem=16, scratch=(), far_in=(), far_out=()
):
    count, waits = len(args), len(after) + len(behind)
    near = pl.BlockSpec(memory_space=pltpu.VMEM)
    outs = out_shape if isinstance(out_shape, list) else [out_shape]
    outs = [pltpu.HBM(o.shape, o.dtype) if i in far_out else o for i, o in enumerate(outs)]
    args = [stay(a) if i in far_in else a for i, a in enumerate(args)]

    def body(*refs):
        kernel(*refs[:count], *refs[count + waits :])

    result = pl.pallas_call(
        body,
        out_shape=outs,
        in_specs=[HBM if i in far_in else near for i in range(count)]
        + [pl.BlockSpec(memory_space=pl.ANY)] * len(after)
        + [HBM] * len(behind),
        out_specs=[HBM if i in far_out else near for i in range(len(outs))],
        scratch_shapes=list(scratch),
        compiler_params=pltpu.CompilerParams(vmem_limit_bytes=vmem << 20),
        cost_estimate=lasts(us),
    )(*args, *after, *[stay(a) for a in behind])
    return list(result) if isinstance(out_shape, list) else result[0]


def stay(array):
    return pltpu.with_memory_space_constraint(array, pltpu.HBM)


def sds(shape, dtype=BF16):
    return jax.ShapeDtypeStruct(shape, dtype)


def iota(shape, dim):
    return lax.broadcasted_iota(jnp.int32, shape, dim)


def mask(cond):
    return jnp.where(cond, 1.0, 0.0).astype(BF16)


def dispatch_kernel(experts, x_ref, gain_ref, cot_ref, idt_ref, gt_ref, send_ref):
    tokens = x_ref.shape[0]
    x = x_ref[...].astype(F32)
    inverse = lax.rsqrt(jnp.mean(x * x, axis=-1, keepdims=True) + EPSILON)
    normed = (x * inverse * gain_ref[...]).astype(BF16)
    e_of = iota((experts, tokens), 0)
    hot = [idt_ref[k : k + 1, :] == e_of for k in range(2)]
    before = mask(iota((tokens, tokens), 0) < iota((tokens, tokens), 1))
    count = dot(mask(hot[0] | hot[1]), before)
    rows = experts * 2 * CAP
    r_of = iota((rows, tokens), 0)
    plain, weighted = None, 0.0
    for k in range(2):
        slot = jnp.sum(jnp.where(hot[k], count, 0.0), axis=0, keepdims=True)
        at = idt_ref[k : k + 1, :] * (2 * CAP) + slot.astype(jnp.int32)
        here = r_of == at
        plain = here if plain is None else plain | here
        g = gt_ref[k : k + 1, :].astype(F32)
        weighted = weighted + jnp.where(r_of == at + CAP, g, 0.0)
    choose = jnp.concatenate([mask(plain), weighted.astype(BF16)], axis=1)
    sources = jnp.concatenate([normed, cot_ref[...]], axis=0)
    send_ref[...] = dot(choose, sources).astype(BF16)


def pick(at, weights, after, us):
    _, hid, width = weights[0].shape
    count = len(weights)

    def body(at_ref, *refs):
        out_ref, sems = refs[-2:]
        copies = [
            pltpu.make_async_copy(ref.at[at_ref[0]], out_ref.at[kind], sems.at[kind])
            for kind, ref in enumerate(refs[:count])
        ]
        for copy in copies:
            copy.start()
        for copy in copies:
            copy.wait()

    return pl.pallas_call(
        body,
        in_specs=[pl.BlockSpec(memory_space=pltpu.SMEM)]
        + [HBM] * count
        + [pl.BlockSpec(memory_space=pl.ANY)] * len(after),
        out_specs=pl.BlockSpec(memory_space=pltpu.VMEM),
        out_shape=sds((count, hid, width)),
        scratch_shapes=[pltpu.SemaphoreType.DMA((count,))],
        compiler_params=pltpu.CompilerParams(vmem_limit_bytes=16 << 20),
        cost_estimate=lasts(us),
    )(at, *[stay(w) for w in weights], *after)


def place(at, mine, got, after):
    kinds = len(mine)
    hid, width = mine[0].shape
    moves, kind, row = [], 0, 0
    for part, array in enumerate(got):
        first = 0
        while first < array.shape[0]:
            size = min(hid - row, array.shape[0] - first)
            moves.append((kind, row, part, first, size))
            first, row = first + size, row + size
            if row == hid:
                kind, row = kind + 1, 0
    count = kinds + len(got)

    def body(at_ref, *refs):
        mine_refs, got_refs = refs[:kinds], refs[kinds:count]
        outs, sems = refs[count + len(after) : -1], refs[-1]
        at = at_ref[0]
        copies = []
        for k, out in enumerate(outs):
            copies.append(pltpu.make_async_copy(mine_refs[k], out.at[at], sems.at[k]))
        for i, (k, to, part, first, rows) in enumerate(moves):
            copies.append(
                pltpu.make_async_copy(
                    got_refs[part].at[pl.ds(first, rows), :],
                    outs[k].at[1 - at, pl.ds(to, rows), :],
                    sems.at[kinds + i],
                )
            )
        for copy in copies:
            copy.start()
        for copy in copies:
            copy.wait()

    return pl.pallas_call(
        body,
        out_shape=[pltpu.HBM((2, hid, width), BF16)] * kinds,
        in_specs=[pl.BlockSpec(memory_space=pltpu.SMEM)]
        + [pl.BlockSpec(memory_space=pltpu.VMEM)] * count
        + [pl.BlockSpec(memory_space=pl.ANY)] * len(after),
        out_specs=[HBM] * kinds,
        scratch_shapes=[pltpu.SemaphoreType.DMA((kinds + len(moves),))],
        compiler_params=pltpu.CompilerParams(vmem_limit_bytes=4 << 20),
        cost_estimate=lasts(3),
    )(at, *mine, *got, *after)


def separate(sx_ref, ss_ref, part_ref, xs_ref, j):
    step = GROUP * CAP
    for i in range(part_ref.shape[0] // (2 * step)):
        block = part_ref[2 * step * i : 2 * step * (i + 1), :]
        at = slice(step * j, step * (j + 1))
        xs_ref[0, at, :] = dot(sx_ref[...], block).astype(BF16)
        xs_ref[1, at, :] = dot(ss_ref[...], block).astype(BF16)
        j += 1
    return j


def hidden_block(xs_ref, w_ref, saved_ref):
    pre_gate = dot(xs_ref[0], w_ref[0], 1, 1)
    pre_up = dot(xs_ref[0], w_ref[1], 1, 1)
    d_hidden = dot(xs_ref[1], w_ref[2], 1, 1)
    cdf = 0.5 * (1.0 + lax.erf(pre_gate * 0.7071067811865476))
    pdf = jnp.exp(-0.5 * pre_gate * pre_gate) * 0.3989422804014327
    activated = pre_gate * cdf
    hidden = (activated * pre_up).astype(BF16)
    d_gate = (d_hidden * pre_up * (cdf + pre_gate * pdf)).astype(BF16)
    d_up = (d_hidden * activated).astype(BF16)
    for kind, value in enumerate((d_gate, d_up, hidden)):
        saved_ref[kind] = value
    rows = dot(d_gate, w_ref[0]) + dot(d_up, w_ref[1])
    return rows, jnp.sum(hidden.astype(F32) * d_hidden, axis=1, keepdims=True)


def put_back(back_ref, total, gate):
    rows = total.shape[0]
    back_ref[:rows, :] = total.astype(BF16)
    spread = jnp.broadcast_to(gate, (rows, 128)).T
    back_ref[rows:, :rows] = spread[:16, :].astype(BF16)
    back_ref[rows:, rows:] = jnp.zeros((16, back_ref.shape[1] - rows), BF16)


def piece_kernel(count, sx_ref, ss_ref, *refs):
    parts, refs = refs[:count], refs[count:]
    blocks = (len(refs) - 6) // 2
    weights, refs = refs[:blocks], refs[blocks:]
    back_ref, xs_out, refs = refs[0], refs[1], refs[2:]
    saved_outs, (part_scr, xs_ref, saved_ref), sems = refs[:blocks], refs[blocks:-1], refs[-1]
    size = parts[0].shape[0]
    fetches = [
        pltpu.make_async_copy(p, part_scr.at[pl.ds(size * i, size), :], sems.at[i])
        for i, p in enumerate(parts)
    ]
    for fetch in fetches:
        fetch.start()
    j = 0
    for i, fetch in enumerate(fetches):
        fetch.wait()
        j = separate(sx_ref, ss_ref, part_scr.at[pl.ds(size * i, size), :], xs_ref, j)
    stores = [pltpu.make_async_copy(xs_ref, xs_out, sems.at[count])]
    stores[0].start()
    total, gate = None, None
    for n, w_ref in enumerate(weights):
        rows, terms = hidden_block(xs_ref, w_ref, saved_ref.at[n])
        stores.append(
            pltpu.make_async_copy(saved_ref.at[n], saved_outs[n], sems.at[count + 1 + n])
        )
        stores[-1].start()
        total = rows if n == 0 else total + rows
        gate = terms if n == 0 else gate + terms
    put_back(back_ref, total, gate)
    for store in stores:
        store.wait()


def second_half_kernel(xs_in, w_ref, part_ref, back_ref, saved_out, xs_ref, saved_ref, sems):
    fetch = pltpu.make_async_copy(xs_in, xs_ref, sems.at[0])
    fetch.start()
    fetch.wait()
    total, gate = hidden_block(xs_ref, w_ref, saved_ref)
    store = pltpu.make_async_copy(saved_ref, saved_out, sems.at[1])
    store.start()
    put_back(back_ref, total, gate)
    back_ref[...] = (back_ref[...].astype(F32) + part_ref[...].astype(F32)).astype(BF16)
    store.wait()


def expert_piece(parts, weights, sel, behind):
    width = parts[0].shape[-1]
    parts = [p.reshape(-1, width) for p in parts]
    rows = sum(p.shape[0] for p in parts) // 2
    hid = weights[0].shape[1]
    blocks, count = len(weights), len(parts)
    return on_chip(
        functools.partial(piece_kernel, count),
        [sds((rows + 16, width)), sds((2, rows, width))] + [sds((3, rows, hid))] * blocks,
        [*sel, *parts, *weights],
        us=0.5,
        vmem=24,
        behind=behind,
        scratch=[
            pltpu.VMEM((2 * rows, width), BF16),
            pltpu.VMEM((2, rows, width), BF16),
            pltpu.VMEM((blocks, 3, rows, hid), BF16),
            pltpu.SemaphoreType.DMA((count + 1 + blocks,)),
        ],
        far_in=range(2, 2 + count),
        far_out=range(1, 2 + blocks),
    )


def second_half(xs, got_w, part, behind):
    saved = (3, xs.shape[1], got_w.shape[1])
    return on_chip(
        second_half_kernel,
        [sds(part.shape), sds(saved)],
        [xs, got_w, part],
        us=0.5,
        behind=behind,
        scratch=[
            pltpu.VMEM(xs.shape, BF16),
            pltpu.VMEM(saved, BF16),
            pltpu.SemaphoreType.DMA((2,)),
        ],
        far_in=(0,),
        far_out=(1,),
    )


def weight_kernel(n, hid, kinds, *refs):
    count = len(kinds)
    ins, outs = refs[: 2 * n], refs[2 * n : -3]
    xs_ref, saved_ref, sems = refs[-3:]
    low, high = kinds[0] // 2, kinds[-1] // 2
    rows = saved_ref.shape[1] // n
    fetches = []
    for z in range(n):
        at = pl.ds(rows * z, rows)
        moves = (
            (ins[2 * z].at[pl.ds(low, high + 1 - low)], xs_ref),
            (ins[2 * z + 1].at[pl.ds(kinds[0], count)], saved_ref),
        )
        for i, (src, ref) in enumerate(moves):
            fetches.append(pltpu.make_async_copy(src, ref.at[:, at, :], sems.at[2 * z + i]))
            fetches[-1].start()
    for fetch in fetches:
        fetch.wait()
    part, to = 0, 0
    for i, kind in enumerate(kinds):
        total = dot(saved_ref[i], xs_ref[kind // 2 - low], 0, 0).astype(BF16)
        at = 0
        while at < hid:
            size = min(hid - at, outs[part].shape[0] - to)
            outs[part][to : to + size, :] = total[at : at + size, :]
            at, to = at + size, to + size
            if to == outs[part].shape[0]:
                part, to = part + 1, 0


def weight_grads(results, half, hid, kinds, parts, after):
    xs, saved = results[0][1:3]
    n, (_, rows, padded), width = len(results), saved.shape, xs.shape[2]
    count = len(kinds)
    inputs = kinds[-1] // 2 + 1 - kinds[0] // 2
    return on_chip(
        functools.partial(weight_kernel, n, hid, kinds),
        [sds((part, width)) for part in parts],
        [a for r in results for a in (r[1], r[2 + half])],
        us=0.5,
        vmem=16,
        after=after,
        scratch=[
            pltpu.VMEM((inputs, n * rows, width), BF16),
            pltpu.VMEM((count, n * rows, padded), BF16),
            pltpu.SemaphoreType.DMA((2 * n,)),
        ],
        far_in=range(2 * n),
    )


def payload_kernel(spread_ref, ga_ref, gb_ref, xs_ref, a_ref, b_ref, c_ref, d_ref, out_ref):
    rows = a_ref.shape[0] - 16
    step = GROUP * CAP
    total = (a_ref[...].astype(F32) + b_ref[...].astype(F32)) + (
        c_ref[...].astype(F32) + d_ref[...].astype(F32)
    )
    gates = total[rows : rows + 1, :rows]
    total = total[:rows, :]
    gain = jnp.sum(total * xs_ref[0].astype(F32), axis=0, keepdims=True)
    coarse = gain.astype(BF16)
    fine = (gain - coarse.astype(F32)).astype(BF16)
    order = iota((16, gain.shape[1]), 0)
    gains = jnp.where(order == 0, coarse.astype(F32), 0.0) + jnp.where(
        order == 1, fine.astype(F32), 0.0
    )
    gains = gains.astype(BF16)
    total = total.astype(BF16)
    wide = GROUP * BACK
    for j in range(rows // step):
        block = jnp.concatenate([total[step * j : step * (j + 1), :], gains], axis=0)
        out_ref[wide * j : wide * (j + 1), :] = dot(spread_ref[...], block).astype(BF16)
    placed = dot((ga_ref[...].astype(F32) * gates).astype(BF16), gb_ref[...]).astype(BF16)
    out_ref[:, :128] = out_ref[:, :128] + placed


def column(row):
    count = row.shape[1]
    return jnp.broadcast_to(row, (count, count)).T[:, :1]


def combine_kernel(
    experts, r_ref, x_ref, gain_ref, cot_ref, idt_ref, gt_ref, out_ref, heads_ref, gain_out, gates_out
):
    tokens = x_ref.shape[0]
    e_of = iota((tokens, experts), 1)
    ids = [column(idt_ref[k : k + 1, :].astype(F32)).astype(jnp.int32) for k in range(2)]
    hot = [i == e_of for i in ids]
    before = mask(iota((tokens, tokens), 1) < iota((tokens, tokens), 0))
    count = dot(before, mask(hot[0] | hot[1]))
    slots = [
        jnp.sum(jnp.where(h, count, 0.0), axis=1, keepdims=True).astype(jnp.int32) for h in hot
    ]
    r_of = iota((tokens, experts * BACK), 1)
    take = mask((r_of == ids[0] * BACK + slots[0]) | (r_of == ids[1] * BACK + slots[1]))
    d_normed = dot(take, r_ref[...])
    lane = iota((tokens, 128), 1)
    for k in range(2):
        line = dot(mask(r_of == ids[k] * BACK + CAP), r_ref[:, :128])
        found = jnp.sum(jnp.where(lane == slots[k], line, 0.0), axis=1, keepdims=True)
        gates_out[:, k : k + 1] = found / column(gt_ref[k : k + 1, :].astype(F32))
    gain = gain_ref[...]
    line_of = iota((16, experts * BACK), 1) % BACK
    sums = dot(mask((line_of == CAP + 1) | (line_of == CAP + 2)), r_ref[...])
    gain_out[...] = sums[:1, :] / gain
    x = x_ref[...].astype(F32)
    inverse = lax.rsqrt(jnp.mean(x * x, axis=-1, keepdims=True) + EPSILON)
    unit = x * inverse
    scaled = d_normed * gain
    grad = cot_ref[...].astype(F32) + inverse * (
        scaled - unit * jnp.mean(scaled * unit, axis=-1, keepdims=True)
    )
    grad = grad.astype(BF16)
    out_ref[...] = grad
    put_heads(heads_ref, 0, grad)


def put_heads(out_ref, offset, rows):
    half = rows.shape[0] // 2
    count = rows.shape[1] // 128
    for pair in range(2):
        for head in range(count):
            out_ref[pair * count + head, offset : offset + half, :] = rows[
                pair * half : (pair + 1) * half, head * 128 : (head + 1) * 128
            ]


def pack_kernel(*refs):
    srcs, out_ref, held, sems = refs[:3], refs[3], refs[4:7], refs[7]
    fetches = [
        pltpu.make_async_copy(src, ref, sems.at[i]) for i, (src, ref) in enumerate(zip(srcs, held))
    ]
    for fetch in fetches:
        fetch.start()
    offset = 0
    for fetch, ref in zip(fetches, held):
        fetch.wait()
        put_heads(out_ref, offset, ref)
        offset += ref.shape[0] // 2


def pack(arrays, after):
    rows = sum(a.shape[0] for a in arrays) // 2
    width = arrays[0].shape[1]
    return on_chip(
        pack_kernel,
        sds((2 * width // 128, rows, 128)),
        arrays,
        us=0.5,
        after=after,
        scratch=[pltpu.VMEM(a.shape, BF16) for a in arrays] + [pltpu.SemaphoreType.DMA((3,))],
        far_in=range(3),
    )


def unpack_kernel(in_ref, *outs):
    offset = 0
    for ref in outs:
        half = ref.shape[0] // 2
        count = ref.shape[1] // 128
        for pair in range(2):
            for head in range(count):
                ref[pair * half : (pair + 1) * half, head * 128 : (head + 1) * 128] = in_ref[
                    pair * count + head, offset : offset + half, :
                ]
        offset += half


def cut_kernel(prev_ref, next_ref, low_ref, high_ref):
    half = low_ref.shape[0]
    low_ref[...] = prev_ref[:half]
    high_ref[...] = next_ref[half:]


def attn_forward_kernel(n_q, n_m, scale, b, qkv_ref, p_out, o_ref, s_scr, p_ref, sems):
    seq = qkv_ref.shape[0]
    lq = seq * n_q
    per = 2
    chunk = per * n_m
    count = seq // per
    q = qkv_ref[:, pl.ds(b * n_q, n_q), :].reshape(lq, 128)
    qt = (q.astype(F32) * scale).T
    half_of = iota((128, lq), 0) < 64
    k_at = 2 * n_q + b * n_m
    v_at = 2 * n_q + 2 * n_m + b * n_m
    for h in range(2):
        qh = jnp.where(half_of if h == 0 else jnp.logical_not(half_of), qt, 0.0).astype(BF16)

        def score(c, peak):
            k = qkv_ref[pl.ds(c * per, per), pl.ds(k_at, n_m), :].reshape(chunk, 128)
            s = dot(k, qh)
            s_scr[pl.ds(pl.multiple_of(c * chunk, chunk), chunk), :] = s
            return jnp.maximum(peak, jnp.max(s, axis=0, keepdims=True))

        peak = lax.fori_loop(0, count, score, jnp.full((1, lq), -jnp.inf, F32))

        def power(c, total):
            at = pl.ds(pl.multiple_of(c * chunk, chunk), chunk)
            e = jnp.exp(s_scr[at, :] - peak)
            s_scr[at, :] = e
            return total + jnp.sum(e, axis=0, keepdims=True)

        total = lax.fori_loop(0, count, power, jnp.zeros((1, lq), F32))
        factor = 1.0 / total

        def finish(c, out):
            at = pl.ds(pl.multiple_of(c * chunk, chunk), chunk)
            p = (s_scr[at, :] * factor).astype(BF16)
            p_ref[h, at, :] = p
            v = qkv_ref[pl.ds(c * per, per), pl.ds(v_at, n_m), :].reshape(chunk, 128)
            vt = v.astype(F32).T.astype(BF16)
            return out + dot(vt[64 * h : 64 * h + 64, :], p)

        o_ref[64 * h : 64 * h + 64, :] = lax.fori_loop(
            0, count, finish, jnp.zeros((64, lq), F32)
        )
        pltpu.make_async_copy(p_ref.at[h], p_out.at[h], sems.at[h]).start()
    for h in range(2):
        pltpu.make_async_copy(p_ref.at[h], p_out.at[h], sems.at[h]).wait()


def attn_backward_kernel(
    n_q, n_m, scale, qkv_ref, do_ref, p0_ref, p1_ref, o0_ref, o1_ref, out_ref, dq_scr, p_scr, sems
):
    seq = qkv_ref.shape[0]
    lq = seq * n_q
    per = 4
    chunk = per * n_m
    lane = iota((lq, 128), 1) < 64
    row = iota((128, lq), 0) < 64
    zero = jnp.zeros((), BF16)
    p_refs = (p0_ref, p1_ref)

    def fetch(b, c):
        at = pl.ds(c * chunk, chunk)
        return pltpu.make_async_copy(p_refs[b].at[:, at, :], p_scr.at[b, :, at, :], sems.at[b, c])

    for b in range(2):
        for c in range(seq // per):
            fetch(b, c).start()
    for b, o_ref in enumerate((o0_ref, o1_ref)):
        q_at = pl.ds(b * n_q, n_q)
        k_at = pl.ds(2 * n_q + b * n_m, n_m)
        v_at = pl.ds(2 * n_q + 2 * n_m + b * n_m, n_m)
        d_out = do_ref[:, q_at, :].reshape(lq, 128)
        dt = d_out.astype(F32).T
        prod = dt * o_ref[...]
        delta = [jnp.sum(prod[64 * h : 64 * h + 64, :], axis=0, keepdims=True) for h in range(2)]
        dt = dt.astype(BF16)
        q = (qkv_ref[:, q_at, :].reshape(lq, 128).astype(F32) * scale).astype(BF16)
        rows_of = [jnp.where(row, dt, zero), jnp.where(row, zero, dt)]
        d_out_of = [jnp.where(lane, d_out, zero), jnp.where(lane, zero, d_out)]
        q_of = [jnp.where(lane, q, zero), jnp.where(lane, zero, q)]
        dq_scr[...] = jnp.zeros_like(dq_scr)

        for c in range(seq // per):
            src = pl.ds(c * per, per)
            at = pl.ds(c * chunk, chunk)
            fetch(b, c).wait()
            k = qkv_ref[src, k_at, :].reshape(chunk, 128)
            v = qkv_ref[src, v_at, :].reshape(chunk, 128)
            kt = k.astype(F32).T.astype(BF16)
            dk, dv = None, None
            for h in range(2):
                d_p = dot(v, rows_of[h])
                p = p_scr[b, h, at, :]
                ds = (p.astype(F32) * (d_p - delta[h])).astype(BF16)
                dv_h = dot(p, d_out_of[h])
                dk_h = dot(ds, q_of[h])
                dv = dv_h if dv is None else dv + dv_h
                dk = dk_h if dk is None else dk + dk_h
                mine = slice(64 * h, 64 * h + 64)
                dq_scr[mine, :] += dot(kt[mine, :], ds)
            out_ref[src, k_at, :] = dk.astype(BF16).reshape(per, n_m, 128)
            out_ref[src, v_at, :] = dv.astype(BF16).reshape(per, n_m, 128)
        dq = (dq_scr[...] * scale).T.astype(BF16)
        out_ref[:, q_at, :] = dq.reshape(seq, n_q, 128)


def attn_forward(qkv, example, n_q, n_m, scale, after):
    seq = qkv.shape[0]
    lq, lm = seq * n_q, seq * n_m
    return on_chip(
        functools.partial(attn_forward_kernel, n_q, n_m, scale, example),
        [sds((2, lm, lq)), sds((128, lq), F32)],
        [qkv],
        us=8.7,
        after=after,
        scratch=[
            pltpu.VMEM((lm, lq), F32),
            pltpu.VMEM((2, lm, lq), BF16),
            pltpu.SemaphoreType.DMA((2,)),
        ],
        far_out=(0,),
    )


def attn_backward(qkv, d_out, probs, o_t, n_q, n_m, scale, after):
    seq = qkv.shape[0]
    lq = seq * n_q
    return on_chip(
        functools.partial(attn_backward_kernel, n_q, n_m, scale),
        sds(qkv.shape),
        [qkv, d_out, *probs, *o_t],
        us=11,
        after=after,
        vmem=24,
        scratch=[
            pltpu.VMEM((128, lq), F32),
            pltpu.VMEM((2, 2, seq * n_m, lq), BF16),
            pltpu.SemaphoreType.DMA((2, seq // 4)),
        ],
        far_in=(2, 3),
    )


def selections(experts):
    r = np.arange(GROUP * CAP)
    c = np.arange(2 * GROUP * CAP)
    first = c[None, :] == ((r // CAP) * 2 * CAP + r % CAP)[:, None]
    second = c[None, :] == ((r // CAP) * 2 * CAP + r % CAP + CAP)[:, None]
    o = np.arange(GROUP * BACK)
    spread = (r[None, :] == ((o // BACK) * CAP + o % BACK)[:, None]) & (o % BACK < CAP)[:, None]
    extra = (o % BACK)[:, None] == (CAP + 1 + np.arange(16))[None, :]
    spread = np.concatenate([spread, extra], axis=1)
    o_all = np.arange(experts * BACK)
    c_all = np.arange(experts * CAP)
    lines = (o_all % BACK == CAP)[:, None] & (c_all[None, :] // CAP == o_all[:, None] // BACK)
    lanes = c_all[:, None] % CAP == np.arange(128)[None, :]
    return [jnp.asarray(m.astype(np.float32), BF16) for m in (first, second, spread, lines, lanes)]


def on_device(
    queries,
    memory_keys,
    memory_values,
    stream,
    norm_gain,
    gate_proj,
    up_proj,
    down_proj,
    expert_ids,
    gate_weights,
    upstream_grad,
):
    examples, positions, width = stream.shape
    mem_rows = memory_keys.shape[1]
    tokens = examples * positions
    experts = lax.axis_size("seq") * gate_proj.shape[0]
    logit_scale = (width // HEADS) ** (-0.5)
    my_dp = lax.axis_index("dp")
    sel_x, sel_s, spread, lines, lanes = selections(experts)

    w_t = [jnp.swapaxes(gate_proj, 1, 2), jnp.swapaxes(up_proj, 1, 2), down_proj]
    hid = w_t[2].shape[1]
    at = my_dp.reshape(1).astype(jnp.int32)
    give_w = pick(1 - at, w_t, [], 1)
    got_w = xor_swap(give_w, "dp", 1)

    x_rows = stream.reshape(tokens, width)
    cot_rows = upstream_grad.reshape(tokens, width)
    gain_row = norm_gain.reshape(1, width)
    ids = expert_ids.reshape(tokens, 2).T
    gates = gate_weights.reshape(tokens, 2).T
    send = on_chip(
        functools.partial(dispatch_kernel, experts),
        sds((experts * 2 * CAP, width)),
        [x_rows, gain_row, cot_rows, ids, gates],
        us=2.5,
        after=[give_w],
    )
    arrived = lax.all_to_all(
        send.reshape(experts, 2 * CAP, width), ("seq", "dp"), 0, 0, tiled=True
    )
    own_w = pick(at, w_t, [send], 1)

    from_prev = shift(arrived, "expert", 1)
    from_next = shift(arrived, "expert", -1)
    cut = experts // 2
    sel = (sel_x, sel_s)
    n_q, n_m = positions, mem_rows
    own_half = expert_piece([arrived], [own_w], sel, [])
    packed = pack(
        [a.reshape(-1, width) for a in (queries, memory_keys, memory_values)], [own_half[0]]
    )
    relays = on_chip(
        cut_kernel,
        [sds((cut, 2 * CAP, width))] * 2,
        [from_prev, from_next],
        us=0.5,
        after=[packed, got_w],
    )
    far = [shift(relays[0], "expert", 1), shift(relays[1], "expert", -1)]
    packed, first_cut = lax.optimization_barrier((packed, relays[0]))
    after = [first_cut]
    qkv = lax.all_to_all(packed, "seq", 0, 0, tiled=True)
    results = []
    for part in (from_prev, from_next):
        results.append(expert_piece([part], [own_w, got_w], sel, after))
        after = [results[-1][1]]
    back, saved2 = second_half(own_half[1], got_w, own_half[0], after)
    results.append((back, *own_half[1:], saved2))
    results.append(expert_piece(far, [own_w, got_w], sel, [saved2]))
    backs = [
        shift(res[0], "expert", -by) if by else res[0]
        for by, res in zip((1, -1, 0, 2), results)
    ]
    theirs = weight_grads(results, 1, hid, (0,), (hid,), [])
    got_grads = [xor_swap(theirs[0], "dp", 1)]
    theirs += weight_grads(results, 1, hid, (1, 2), (hid, hid // 2, hid // 2), theirs)
    payload = on_chip(
        payload_kernel,
        sds((experts * BACK, width)),
        [spread, lines, lanes, results[2][1], *backs],
        us=2,
        after=[theirs[1], got_grads[0]],
    )
    payload, send_grads = lax.optimization_barrier((payload, theirs[1]))
    got_grads.append(xor_swap(send_grads, "dp", 1))
    returned = lax.all_to_all(
        payload.reshape(experts, BACK, width), ("seq", "dp"), 0, 0, tiled=True
    )
    probs0, o0 = attn_forward(qkv, 0, n_q, n_m, logit_scale, [payload])
    probs1, o1 = attn_forward(qkv, 1, n_q, n_m, logit_scale, [o0])

    stream_grad, heads_grad, gain_grad, gates_grad = on_chip(
        functools.partial(combine_kernel, experts),
        [
            sds((tokens, width)),
            sds((2 * width // 128, tokens // 2, 128)),
            sds((1, width), F32),
            sds((tokens, 2), F32),
        ],
        [returned.reshape(experts * BACK, width), x_rows, gain_row, cot_rows, ids, gates],
        us=2,
        after=[o1, got_grads[1]],
    )
    heads_grad = lax.all_to_all(heads_grad, "seq", 0, 0, tiled=True)
    heads_grad, *send_grads = lax.optimization_barrier((heads_grad, theirs[2], theirs[3]))
    got_grads += [xor_swap(part, "dp", 1) for part in send_grads]
    for bits in (1, 2):
        gain_grad = gain_grad + xor_swap(gain_grad, "expert", bits)

    out = attn_backward(
        qkv, heads_grad, (probs0, probs1), (o0, o1), n_q, n_m, logit_scale, []
    )
    out, got_grads[2], got_grads[3] = lax.optimization_barrier((out, got_grads[2], got_grads[3]))
    mine = weight_grads(results, 0, hid, (0, 1, 2), (hid,) * 3, [out])
    w_grads = place(at, mine, got_grads, [])
    w_grads = [jnp.swapaxes(w_grads[0], 1, 2), jnp.swapaxes(w_grads[1], 1, 2), w_grads[2]]
    out = lax.all_to_all(out, "seq", 0, 0, tiled=True)
    shapes = [(examples * n, width) for n in (n_q, n_m, n_m)]
    d_q, d_k, d_v = on_chip(unpack_kernel, [sds(s) for s in shapes], [out], us=2)
    return (
        d_q.reshape(queries.shape),
        d_k.reshape(memory_keys.shape),
        d_v.reshape(memory_values.shape),
        stream_grad.reshape(stream.shape),
        gain_grad.reshape(width),
        *w_grads,
        gates_grad.reshape(gate_weights.shape),
    )


def solution(mesh):
    rows = P(("expert", "dp"), "seq", None)
    wide = P("seq", None, ("expert", "dp"))
    deep = P("seq", ("expert", "dp"), None)
    pairs = P("seq", ("expert", "dp"), None, None)
    in_specs = (rows, rows, rows, rows, P(), wide, wide, deep, pairs, pairs, rows)
    out_specs = (rows, rows, rows, rows, P(), wide, wide, deep, pairs)
    return jax.shard_map(
        on_device, mesh=mesh, in_specs=in_specs, out_specs=out_specs, check_vma=False
    )
```
